32 devices in a mesh: wide: 8 (over z, y), narrow: 4 (over x, core).
Axes of the slice: x: 2, y: 2, z: 4, core: 2. Of those that a mesh axis runs over, the one named last changes fastest.
Arguments:
- tokens: bfloat16 [32, 1024, 768], P(('wide', 'narrow')), may hold values from -6 to 6
- first_values: bfloat16 [32, 1024, 384], P(('wide', 'narrow')), may hold values from -6 to 6
- cotangent: bfloat16 [32, 1024, 768], P(('wide', 'narrow')), may hold values from -6 to 6
- lengths: int32 [32], P(('wide', 'narrow')), may hold values from 1 to 1024, 16384 in all
- weight_in: float32 [768, 1920], P(('wide', 'narrow')), may hold values from -0.21875 to 0.21875
- weight_out: float32 [768, 768], P(('wide', 'narrow')), may hold values from -1.75 to 1.75
- weight_up: float32 [768, 3072], P(('wide', 'narrow')), may hold values from -0.21875 to 0.21875
- weight_down: float32 [3072, 768], P(('wide', 'narrow')), may hold values from -0.109375 to 0.109375
- first_in: float32 [768, 1920], P(('wide', 'narrow')), may hold values from -0.0015348548 to 0.0015348548
- first_out: float32 [768, 768], P(('wide', 'narrow')), may hold values from -0.0015348548 to 0.0015348548
- first_up: float32 [768, 3072], P(('wide', 'narrow')), may hold values from -0.0015348548 to 0.0015348548
- first_down: float32 [3072, 768], P(('wide', 'narrow')), may hold values from -0.0015348548 to 0.0015348548
- second_in: float32 [768, 1920], P(('wide', 'narrow')), may hold values from 1.472362e-07 to 5.889448e-07
- second_out: float32 [768, 768], P(('wide', 'narrow')), may hold values from 1.472362e-07 to 5.889448e-07
- second_up: float32 [768, 3072], P(('wide', 'narrow')), may hold values from 1.472362e-07 to 5.889448e-07
- second_down: float32 [3072, 768], P(('wide', 'narrow')), may hold values from 1.472362e-07 to 5.889448e-07
- shadow_in: float32 [768, 1920], P(('wide', 'narrow')), may hold values from -0.21875 to 0.21875
- shadow_out: float32 [768, 768], P(('wide', 'narrow')), may hold values from -1.75 to 1.75
- shadow_up: float32 [768, 3072], P(('wide', 'narrow')), may hold values from -0.21875 to 0.21875
- shadow_down: float32 [3072, 768], P(('wide', 'narrow')), may hold values from -0.109375 to 0.109375
- vectors: float32 [8832], replicated, as said below
- first_vectors: float32 [8832], replicated, may hold values from -0.006139419 to 0.006139419
- second_vectors: float32 [8832], replicated, may hold values from 2.355779e-06 to 9.423116e-06
- shadow_vectors: float32 [8832], replicated, may hold values from 0.5 to 1.5
Outputs:
- result: bfloat16 [32, 1024, 768], P(('wide', 'narrow'))
- grad_tokens: bfloat16 [32, 1024, 768], P(('wide', 'narrow'))
- grad_values: bfloat16 [32, 1024, 384], P(('wide', 'narrow'))
- grad_norm: float32 [], replicated
- updated_in: float32 [768, 1920], P(('wide', 'narrow'))
- moment_in: float32 [768, 1920], P(('wide', 'narrow'))
- square_in: float32 [768, 1920], P(('wide', 'narrow'))
- average_in: float32 [768, 1920], P(('wide', 'narrow'))
- updated_out: float32 [768, 768], P(('wide', 'narrow'))
- moment_out: float32 [768, 768], P(('wide', 'narrow'))
- square_out: float32 [768, 768], P(('wide', 'narrow'))
- average_out: float32 [768, 768], P(('wide', 'narrow'))
- updated_up: float32 [768, 3072], P(('wide', 'narrow'))
- moment_up: float32 [768, 3072], P(('wide', 'narrow'))
- square_up: float32 [768, 3072], P(('wide', 'narrow'))
- average_up: float32 [768, 3072], P(('wide', 'narrow'))
- updated_down: float32 [3072, 768], P(('wide', 'narrow'))
- moment_down: float32 [3072, 768], P(('wide', 'narrow'))
- square_down: float32 [3072, 768], P(('wide', 'narrow'))
- average_down: float32 [3072, 768], P(('wide', 'narrow'))
- updated_vectors: float32 [8832], replicated
- moment_vectors: float32 [8832], replicated
- square_vectors: float32 [8832], replicated
- average_vectors: float32 [8832], replicated
The draws below stay inside these ranges and needn't reach their ends.
Inputs may be any that keep to these rules, and one draw needn't show every extreme that they name: `lengths`: the longest sequence has exactly 1024 real tokens; positions from a sequence's length on are padding. `vectors`: laid end to end: first norm's gain and shift, second norm's gain and shift, query bias, fresh value bias, output projection bias, hidden bias, down projection bias.
All inputs are finite; a program needn't handle non-finite values. No bound on the sum of `lengths` on one device may be relied on, other than what follows from the above.
Results may differ from the reference program's by a relative error of at most 0.013.
The reference program's roundings to bfloat16 on the way count: a program that leaves them out, or rounds other values in their place, can miss the bound.
Values may be sent and summed in bfloat16 or wider, within the bound.
A program may use at most 256 MiB of HBM per device.

```python
import math
import jax
import jax.numpy as jnp
import numpy as np
from jax import lax

D = 768
H = 12
HD = 64
FF = 3072
VH = 6
SEQ_LEN = 1024
STEP = 7
SEQS = 32
VEC = 8832
NPARAM = 6791808


def draw_vectors(key, part):
    key = jax.random.fold_in(key, 11)
    key_gain = jax.random.fold_in(key, 1)
    key_bias = jax.random.fold_in(key, 2)
    ramp = jnp.linspace(0.6, 1.8, D, dtype=jnp.float32)
    biases = 0.2 * jax.random.normal(key_bias, (VEC - 2 * D,), jnp.float32)
    jitter = jax.random.uniform(key_gain, (2, D), jnp.float32, 0.8, 1.2)
    gains = ramp[None, :] * jitter
    return jnp.concatenate([gains[0], biases[:D], gains[1], biases[D:]]).astype(jnp.float32)


def with_spikes(values, stream_key, source, target, parts, factor):
    def block_of(axis_at):
        return (jnp.arange(values.shape[axis_at]) // (values.shape[axis_at] // parts)).reshape((-1,) + (1,) * (values.ndim - 1 - axis_at))

    one_side = jax.random.permutation(stream_key, parts)[block_of(target)]
    far = (block_of(target) + parts // 2) % parts
    return jnp.where((block_of(source) == one_side) | (block_of(source) == far), factor * values, values)


def level_of(rng, shape, cuts, smallest, top_value):
    def one(position, parts):
        steps = jax.random.uniform(jax.random.fold_in(jax.random.fold_in(rng, 6), position), (parts,), jnp.float32, smallest / len(cuts), top_value / len(cuts))
        return jnp.repeat(jnp.exp(steps), shape[position] // parts).reshape((-1,) + (1,) * (len(shape) - position - 1))

    level = one(*cuts[0])
    for cut in cuts[1:]:
        level = level * one(*cut)
    return level


def split_up(amount, total, most, lean):
    weights = [(1 << 20) // math.isqrt(grade ** lean) + 1 for grade in range(2, amount + 1)]
    surplus, counts = total - most - (amount - 1), [1] * (amount - 1)
    while surplus > 0:
        candidates = [i for i in range(amount - 1) if counts[i] < most]
        mass, left = sum([weights[i] for i in candidates]), surplus
        for i in candidates:
            more = min(most - counts[i], max(1, left * weights[i] // mass), surplus)
            counts[i] = counts[i] + more
            surplus = surplus - more
    return np.array([most] + counts)


def uneven_parts(rng, number_of, total, most, lean):
    if number_of == 2:
        one = jax.random.randint(rng, (), max(1, total - most), min(most, total - 1) + 1)
        return jnp.stack([one, total - one])
    tallies = jnp.asarray(split_up(number_of, total, most, lean), jnp.int32)
    twos = (number_of - 1) // 2
    source_of, receiver = tallies[1:1 + 2 * twos:2], tallies[2:2 + 2 * twos:2]
    room = jnp.minimum(source_of - 1, most - receiver)
    moved = jax.random.randint(jax.random.fold_in(rng, 1), (twos,), 0, 1 << 20) % (room + 1)
    tallies = tallies.at[1:1 + 2 * twos:2].set(source_of - moved).at[2:2 + 2 * twos:2].set(receiver + moved)
    return tallies[jax.random.permutation(jax.random.fold_in(rng, 2), number_of)]


def bell_draw(stream_key, shape, width, limit, cuts=(), kind=jnp.bfloat16):
    loudness = level_of(stream_key, shape, cuts, -0.22, 0.18) if cuts else 1.0
    values = jax.random.normal(stream_key, shape, jnp.float32) * width * loudness
    return jnp.minimum(jnp.maximum(values, -limit), limit).astype(kind)


def heavy_noise(rng, shape, deviation, reach, cuts, heavy, kind=jnp.bfloat16):
    values = deviation * jax.random.normal(rng, shape, jnp.float32)
    if cuts:
        values = values * level_of(rng, shape, cuts, -0.22, 0.18)
    return jnp.clip(with_spikes(values, jax.random.fold_in(rng, 3), *heavy), -reach, reach).astype(kind)


def setup_inputs(seed: int = 0) -> dict:
    arg_keys = jax.random.split(jax.random.key(seed), 25)
    return {
        "tokens": bell_draw(arg_keys[0], (SEQS, SEQ_LEN, D), 1.0, 6.0, ((0, 32),)),
        "first_values": bell_draw(arg_keys[1], (SEQS, SEQ_LEN, VH * HD), 1.0, 6.0, ((0, 32),)),
        "cotangent": heavy_noise(arg_keys[2], (SEQS, SEQ_LEN, D), 1.0, 6.0, ((0, 32),), (0, 2, 32, 2.75)),
        "lengths": uneven_parts(arg_keys[3], SEQS, SEQS * SEQ_LEN // 2, SEQ_LEN, 1).astype(jnp.int32),
        "weight_in": bell_draw(arg_keys[4], (D, 2 * H * HD + VH * HD), D ** -0.5, 0.21875, ((0, 32),), jnp.float32),
        "weight_out": bell_draw(arg_keys[5], (H * HD, D), (max(1, H * HD * 16 // SEQ_LEN)) ** -0.5, 1.75, ((0, 32),), jnp.float32),
        "weight_up": bell_draw(arg_keys[6], (D, FF), D ** -0.5, 0.21875, ((0, 32),), jnp.float32),
        "weight_down": bell_draw(arg_keys[7], (FF, D), FF ** -0.5, 0.109375, ((0, 32),), jnp.float32),
        "first_in": bell_draw(arg_keys[8], (D, 2 * H * HD + VH * HD), (1.0 / NPARAM ** 0.5), 0.0015348548, ((0, 32),), jnp.float32),
        "first_out": bell_draw(arg_keys[9], (H * HD, D), (1.0 / NPARAM ** 0.5), 0.0015348548, ((0, 32),), jnp.float32),
        "first_up": bell_draw(arg_keys[10], (D, FF), (1.0 / NPARAM ** 0.5), 0.0015348548, ((0, 32),), jnp.float32),
        "first_down": bell_draw(arg_keys[11], (FF, D), (1.0 / NPARAM ** 0.5), 0.0015348548, ((0, 32),), jnp.float32),
        "second_in": jnp.clip(jnp.exp(math.log(5.889447720619501e-07) - 1.3862944 * jax.random.uniform(arg_keys[12], (D, 2 * H * HD + VH * HD), jnp.float32) ** level_of(arg_keys[12], (D, 2 * H * HD + VH * HD), ((0, 32),), -0.2, 0.2)), 1.4723619301548752e-07, 5.889447720619501e-07),
        "second_out": jnp.clip(jnp.exp(math.log(5.889447720619501e-07) - 1.3862944 * jax.random.uniform(arg_keys[13], (H * HD, D), jnp.float32) ** level_of(arg_keys[13], (H * HD, D), ((0, 32),), -0.2, 0.2)), 1.4723619301548752e-07, 5.889447720619501e-07),
        "second_up": jnp.clip(jnp.exp(math.log(5.889447720619501e-07) - 1.3862944 * jax.random.uniform(arg_keys[14], (D, FF), jnp.float32) ** level_of(arg_keys[14], (D, FF), ((0, 32),), -0.2, 0.2)), 1.4723619301548752e-07, 5.889447720619501e-07),
        "second_down": jnp.clip(jnp.exp(math.log(5.889447720619501e-07) - 1.3862944 * jax.random.uniform(arg_keys[15], (FF, D), jnp.float32) ** level_of(arg_keys[15], (FF, D), ((0, 32),), -0.2, 0.2)), 1.4723619301548752e-07, 5.889447720619501e-07),
        "shadow_in": bell_draw(arg_keys[16], (D, 2 * H * HD + VH * HD), D ** -0.5, 0.21875, ((0, 32),), jnp.float32),
        "shadow_out": bell_draw(arg_keys[17], (H * HD, D), (max(1, H * HD * 16 // SEQ_LEN)) ** -0.5, 1.75, ((0, 32),), jnp.float32),
        "shadow_up": bell_draw(arg_keys[18], (D, FF), D ** -0.5, 0.21875, ((0, 32),), jnp.float32),
        "shadow_down": bell_draw(arg_keys[19], (FF, D), FF ** -0.5, 0.109375, ((0, 32),), jnp.float32),
        "vectors": draw_vectors(jax.random.fold_in(arg_keys[24], 71), 0),
        "first_vectors": bell_draw(arg_keys[21], (VEC,), (4.0 / NPARAM ** 0.5), 0.006139419, (), jnp.float32),
        "second_vectors": jnp.clip(jnp.exp(jax.random.uniform(arg_keys[22], (VEC,), jnp.float32, math.log(2.3557790882478002e-06), math.log(9.423116352991201e-06))), 2.3557790882478002e-06, 9.423116352991201e-06),
        "shadow_vectors": jnp.clip(1.0 + 0.1 * jax.random.normal(arg_keys[23], (VEC,), jnp.float32), 0.5, 1.5),
    }


HIGH = lax.Precision.HIGHEST
BETA_ONE = 0.5
BETA_TWO = 0.5
SHADOW_RATE = 0.5
RATE_MATRIX = 0.03
RATE_OUTPUT = 0.15
RATE_VECTOR = 0.3
DECAY_MATRIX = 0.1
CLIP = 1.0
EPS_ADAM = 1e-08

@jax.custom_vjp
def low(v):
    return lax.optimization_barrier(v.astype(jnp.bfloat16)).astype(jnp.float32)

@jax.custom_vjp
def low_back(v):
    return v

def low_keep(v):
    return (low(v), None)

def low_pass(kept, grad):
    return (grad,)

def back_keep(v):
    return (v, None)

def back_low(kept, grad):
    return (low(grad),)
low.defvjp(low_keep, low_pass)
low_back.defvjp(back_keep, back_low)

def norm_rows(values, gain, shift):
    center = values - lax.optimization_barrier(jnp.mean(values, axis=-1, keepdims=True))
    spread = lax.optimization_barrier(jnp.mean(center * center, axis=-1, keepdims=True))
    return center * lax.rsqrt(spread + 1e-05) * gain + shift

def split_vector(vector):
    extents = [D, D, D, D, H * HD, VH * HD, D, FF, D]
    pieces = []
    offset = 0
    for extent in extents:
        pieces.append(vector[offset:offset + extent])
        offset += extent
    return pieces

def layer(params, inputs, first_f, valid):
    weight_in, weight_out, weight_up, weight_down, vectors = params
    gain_one, shift_one, gain_two, shift_two, bias_query, bias_value, bias_out, bias_up, bias_down = split_vector(vectors)
    groups, seq_len = (inputs.shape[0], inputs.shape[1])
    span = H * HD
    normed = low(norm_rows(inputs, gain_one, shift_one))
    project = jnp.einsum('gtd,de->gte', normed, weight_in, precision=HIGH)
    queries = low(low_back(project[..., :span] + bias_query))
    key_rows = low(low_back(project[..., span:2 * span]))
    fresh = low(low_back(project[..., 2 * span:] + bias_value))
    value_rows = jnp.concatenate([fresh, first_f], axis=-1)
    queries = queries.reshape(groups, seq_len, H, HD)
    key_rows = key_rows.reshape(groups, seq_len, H, HD)
    value_rows = value_rows.reshape(groups, seq_len, H, HD)
    raw = jnp.einsum('gqhe,gkhe->ghqk', queries, key_rows, precision=HIGH) * 0.125
    positions = jnp.arange(seq_len, dtype=jnp.int32)
    causal = positions[None, :] <= positions[:, None]
    allowed = causal[None, None] & (valid[:, None, None, :] > 0.0)
    scores = low_back(jnp.where(allowed, raw, -1000000000.0))
    highest = lax.optimization_barrier(jnp.max(scores, axis=-1, keepdims=True))
    exponent = jnp.exp(scores - highest)
    probs = low(exponent / lax.optimization_barrier(jnp.sum(exponent, axis=-1, keepdims=True)))
    attended = jnp.einsum('ghqk,gkhe->gqhe', probs, value_rows, precision=HIGH)
    attended = low(low_back(attended.reshape(groups, seq_len, span)))
    branch = low_back(jnp.einsum('gte,ed->gtd', attended, weight_out, precision=HIGH) + bias_out)
    middle = inputs + branch
    normed_two = low(norm_rows(middle, gain_two, shift_two))
    hidden_pre = low_back(jnp.einsum('gtd,df->gtf', normed_two, weight_up, precision=HIGH) + bias_up)
    active = low(jax.nn.gelu(hidden_pre, approximate=True))
    feed = low_back(jnp.einsum('gtf,fd->gtd', active, weight_down, precision=HIGH) + bias_down)
    return valid[..., None] * (middle + feed)

def adam_step(master, grad, first, second, shadow, rate, decay):
    moment = BETA_ONE * first + (1.0 - BETA_ONE) * grad
    square = BETA_TWO * second + (1.0 - BETA_TWO) * grad * grad
    moment_hat = moment / (1.0 - BETA_ONE ** STEP)
    square_hat = square / (1.0 - BETA_TWO ** STEP)
    updated = master - rate * (moment_hat / (jnp.sqrt(square_hat) + EPS_ADAM) + decay * master)
    average = SHADOW_RATE * shadow + (1.0 - SHADOW_RATE) * updated
    return (updated, moment, square, average)

def reference(tokens, first_values, cotangent, lengths, weight_in, weight_out, weight_up, weight_down, first_in, first_out, first_up, first_down, second_in, second_out, second_up, second_down, shadow_in, shadow_out, shadow_up, shadow_down, vectors, first_vectors, second_vectors, shadow_vectors):
    masters = (weight_in, weight_out, weight_up, weight_down)
    params = tuple((w.astype(jnp.bfloat16).astype(jnp.float32) for w in masters)) + (vectors,)
    group = math.gcd(SEQS, max(1, 4096 // SEQ_LEN))
    rounds = SEQS // group
    positions = jnp.arange(SEQ_LEN, dtype=jnp.int32)
    valid = (positions[None, :] < lengths[:, None]).astype(jnp.float32)

    def stack(array):
        return array.reshape((rounds, group) + array.shape[1:])

    def step(carry, inputs):
        token_group, value_group, cot_group, valid_group = inputs

        def forward(params_in, token_f, value_f):
            return layer(params_in, token_f, value_f, valid_group)
        outcome, back = jax.vjp(forward, params, token_group.astype(jnp.float32), value_group.astype(jnp.float32))
        grad_params, grad_tok, grad_val = back(cot_group.astype(jnp.float32))
        carry = jax.tree.map(jnp.add, carry, grad_params)
        return (carry, (outcome.astype(jnp.bfloat16), grad_tok.astype(jnp.bfloat16), grad_val.astype(jnp.bfloat16)))
    initial = jax.tree.map(jnp.zeros_like, params)
    totals, stacked = lax.scan(step, initial, (stack(tokens), stack(first_values), stack(cotangent), stack(valid)))
    result = stacked[0].reshape(SEQS, SEQ_LEN, D)
    grad_tokens = stacked[1].reshape(SEQS, SEQ_LEN, D)
    grad_values = stacked[2].reshape(SEQS, SEQ_LEN, VH * HD)
    squares = jnp.float32(0.0)
    for grad in totals:
        squares = squares + jnp.sum(grad * grad)
    grad_norm = jnp.sqrt(squares)
    factor = jnp.minimum(1.0, CLIP / grad_norm)
    firsts = (first_in, first_out, first_up, first_down)
    seconds = (second_in, second_out, second_up, second_down)
    shadows = (shadow_in, shadow_out, shadow_up, shadow_down)
    rates = (RATE_MATRIX, RATE_OUTPUT, RATE_MATRIX, RATE_MATRIX)
    outputs = [result, grad_tokens, grad_values, grad_norm]
    for index in range(4):
        outputs.extend(adam_step(masters[index], factor * totals[index], firsts[index], seconds[index], shadows[index], rates[index], DECAY_MATRIX))
    outputs.extend(adam_step(vectors, factor * totals[4], first_vectors, second_vectors, shadow_vectors, RATE_VECTOR, 0.0))
    return tuple(outputs)
```

```python
import jax
import jax.numpy as jnp
from jax import lax
from jax.experimental import pallas as pl
from jax.experimental.pallas import tpu as pltpu
from jax.sharding import PartitionSpec as P

import functools
bf=jnp.bfloat16; f32=jnp.float32
MESH=pl.DeviceIdType.MESH
D = 768
FF = 3072
WIN=1920; WPAD=2048

class Place:
    def __init__(s):
        s.w=lax.axis_index("wide"); s.n=lax.axis_index("narrow")
        s.z=s.w//2; s.y=s.w%2; s.x=s.n//2; s.c=s.n%2
        s.sib=(s.w,s.n+1-2*s.c); s.xn=(s.w,(s.n+2)%4); s.yn=(s.w+1-2*s.y,s.n)
        s.chip=s.z*4+s.y*2+s.x
    def zdev(s,zt): return (zt*2+s.y,s.n)
    def p(s,zt,dy,dx):
        yy=s.y if not dy else 1-s.y
        xx=s.x if not dx else 1-s.x
        return zt*4+yy*2+xx

def rcopy(src,dst,ss,rs,dev):
    return pltpu.make_async_remote_copy(src_ref=src,dst_ref=dst,send_sem=ss,recv_sem=rs,device_id=dev,device_id_type=MESH)

def entry_barrier(P):
    bar=pltpu.get_barrier_semaphore()
    devs=[P.sib,P.xn,P.yn]
    for d in devs: pl.semaphore_signal(bar,inc=1,device_id=d,device_id_type=MESH)
    for k in (1,2,3):
        pl.semaphore_signal(bar,inc=1,device_id=P.zdev((P.z+k)%4),device_id_type=MESH)
    pl.semaphore_wait(bar,6)

NSEM=16
class Gather:
    def __init__(g,P,W,col0,hc,rb,ss,rs):
        g.P,g.W,g.col0,g.hc,g.rb,g.ss,g.rs=P,W,col0,hc,rb,ss,rs
    def view(g,p,h=None):
        h=g.P.c if h is None else h
        return g.W.at[pl.ds(pl.multiple_of(p*g.rb,g.rb),g.rb),pl.ds(pl.multiple_of(g.col0+h*g.hc,128),g.hc)]
    def half(g,h):
        return g.W.at[:,pl.ds(pl.multiple_of(g.col0+h*g.hc,128),g.hc)]
    def put(g,p,i,dev):
        v=g.view(p); rcopy(v,v,g.ss.at[i],g.rs.at[i],dev).start()
    def got(g,p,i):
        v=g.view(p); rcopy(v,v,g.ss.at[i],g.rs.at[i],g.P.sib).wait_recv()
    def zk(g,k): return (g.P.z+4-k)%4
    def spread(g,p,k):
        g.put(p,3+k,g.P.xn); g.put(p,9+k,g.P.yn); g.put(p,15,g.P.sib)
    def start(g):
        P=g.P; p=P.chip
        for k in (1,2,3): g.put(p,k-1,P.zdev((P.z+k)%4))
        g.spread(p,0)
    def step_z(g):
        for k in (1,2,3):
            p=g.P.p(g.zk(k),0,0)
            g.got(p,k-1); g.spread(p,k)
    def step_xy(g):
        P=g.P
        for k in range(4):
            px=P.p(g.zk(k),0,1); py=P.p(g.zk(k),1,0)
            g.got(px,3+k)
            if k<2: g.put(px,13+k,P.yn)
            g.put(px,15,P.sib)
            g.got(py,9+k)
            if k>=2: g.put(py,5+k,P.xn)
            g.put(py,15,P.sib)
    def step_d(g):
        P=g.P
        for k in range(4):
            pd=P.p(g.zk(k),1,1)
            g.got(pd,13+k if k<2 else 5+k)
            g.put(pd,15,P.sib)
    def finish(g):
        v=g.half(1-g.P.c)
        rcopy(v,v,g.ss.at[15],g.rs.at[15],g.P.sib).wait_recv()
    def drain(g):
        v=g.view(g.P.chip)
        for i in range(15): rcopy(v,v,g.ss.at[i],g.rs.at[i],g.P.sib).wait_send()
        v=g.half(g.P.c)
        rcopy(v,v,g.ss.at[15],g.rs.at[15],g.P.sib).wait_send()

class GatherPlane:
    def __init__(g,P,W,b,hc,rb,ss,rs):
        g.P,g.W,g.b,g.hc,g.rb,g.ss,g.rs=P,W,b,hc,rb,ss,rs
    def view(g,p,part=None):
        r0,n=p*g.rb,g.rb
        if part is not None: n=g.rb//2; r0=r0+part*n
        return g.W.at[pl.ds(pl.multiple_of(r0,n),n),pl.ds(pl.multiple_of(g.P.c*g.hc,128),g.hc)]
    def half(g,h):
        return g.W.at[pl.ds(g.b*4*g.rb,4*g.rb),pl.ds(pl.multiple_of(h*g.hc,128),g.hc)]
    def put(g,p,i,dev,part=None):
        v=g.view(p,part); rcopy(v,v,g.ss.at[i],g.rs.at[i],dev).start()
    def got(g,p,i,part=None):
        v=g.view(p,part); rcopy(v,v,g.ss.at[i],g.rs.at[i],g.P.sib).wait_recv()
    def start(g):
        P=g.P
        @pl.when(P.z==g.b)
        def _():
            for k in (1,2,3): g.put(P.chip,k-1,P.zdev((P.z+k)%4))
    def step_z(g):
        P=g.P; p=P.p(g.b,0,0)
        @pl.when(P.z!=g.b)
        def _():
            k=(P.z+4-g.b)%4
            v=g.view(p); rcopy(v,v,g.ss.at[k-1],g.rs.at[k-1],P.sib).wait_recv()
        g.put(p,3,P.xn); g.put(p,4,P.yn); g.put(p,15,P.sib)
    def step_xy(g):
        P=g.P; px=P.p(g.b,0,1); py=P.p(g.b,1,0)
        g.got(px,3); g.put(px,5,P.yn,0); g.put(px,15,P.sib)
        g.got(py,4); g.put(py,6,P.xn,1); g.put(py,15,P.sib)
    def step_d(g):
        P=g.P; pd=P.p(g.b,1,1)
        g.got(pd,5,0); g.got(pd,6,1); g.put(pd,15,P.sib)
    def finish(g):
        v=g.half(1-g.P.c)
        rcopy(v,v,g.ss.at[15],g.rs.at[15],g.P.sib).wait_recv()
    def drain(g):
        P=g.P; v=g.view(P.chip)
        @pl.when(P.z==g.b)
        def _():
            for i in range(3): rcopy(v,v,g.ss.at[i],g.rs.at[i],P.sib).wait_send()
        for i in (3,4): rcopy(v,v,g.ss.at[i],g.rs.at[i],P.sib).wait_send()
        v=g.view(P.chip,0)
        for i in (5,6): rcopy(v,v,g.ss.at[i],g.rs.at[i],P.sib).wait_send()
        v=g.half(P.c)
        rcopy(v,v,g.ss.at[15],g.rs.at[15],P.sib).wait_send()

def rows(ref,r0,n,c0,m):
    return ref.at[pl.ds(pl.multiple_of(r0,n),n),pl.ds(pl.multiple_of(c0,128),m)]

class Reduce:
    def __init__(g,P,G,col0,hc,rb,R,X,F,ss,rs):
        g.P,g.G,g.col0,g.hc,g.rb,g.R,g.X,g.F,g.ss,g.rs=P,G,col0,hc,rb,R,X,F,ss,rs
    def cs(g,h): return pl.ds(pl.multiple_of(g.col0+h*g.hc,128),g.hc)
    def view(g,p): return g.G.at[pl.ds(pl.multiple_of(p*g.rb,g.rb),g.rb),g.cs(g.P.c)]
    def rs_(g,p): return pl.ds(pl.multiple_of(p*g.rb,g.rb),g.rb)
    def start(g):
        P=g.P
        g.d0=rcopy(g.G.at[:,g.cs(1-P.c)],g.R,g.ss.at[15],g.rs.at[15],P.sib); g.d0.start()
    def put(g,p,i,dev):
        rcopy(g.view(p),g.X.at[i],g.ss.at[i],g.rs.at[i],dev).start()
    def got(g,i):
        v=g.X.at[i]; rcopy(v,v,g.ss.at[i],g.rs.at[i],g.P.sib).wait_recv()
    def addR(g,p):
        g.G[g.rs_(p),g.cs(g.P.c)]=(g.G[g.rs_(p),g.cs(g.P.c)].astype(f32)+g.R[g.rs_(p),:].astype(f32)).astype(bf)
    def step_c(g):
        P=g.P
        g.d0.wait_recv()
        for zt in range(4):
            p=P.p(zt,1,1); g.addR(p)
            g.put(p,zt,P.yn if zt<2 else P.xn)
        for zt in range(4):
            for dy,dx in ((0,1),(1,0),(0,0)): g.addR(P.p(zt,dy,dx))
    def addX(g,p,i):
        g.G[g.rs_(p),g.cs(g.P.c)]=(g.G[g.rs_(p),g.cs(g.P.c)].astype(f32)+g.X[i].astype(f32)).astype(bf)
    def step_d(g):
        P=g.P
        for zt in range(4):
            px=P.p(zt,0,1); py=P.p(zt,1,0)
            g.got(zt)
            if zt<2: g.addX(px,zt)
            else: g.addX(py,zt)
            g.put(px,4+zt,P.xn); g.put(py,8+zt,P.yn)
    def step_xy(g):
        P=g.P
        for k in (1,2,3,0):
            zt=(P.z+k)%4
            v=g.X.at[4+zt]; rcopy(v,v,g.ss.at[4+zt],g.rs.at[4+zt],P.sib).wait_recv()
            v=g.X.at[8+zt]; rcopy(v,v,g.ss.at[8+zt],g.rs.at[8+zt],P.sib).wait_recv()
            p=P.p(zt,0,0)
            s=g.G[g.rs_(p),g.cs(P.c)].astype(f32)+g.X[4+zt].astype(f32)+g.X[8+zt].astype(f32)
            if k:
                g.G[g.rs_(p),g.cs(P.c)]=s.astype(bf)
                g.put(p,11+k,P.zdev(zt))
            else: g.F[...]=s
    def step_z(g):
        s=g.F[...]
        for k in (1,2,3):
            g.got(11+k); s=s+g.X[11+k].astype(f32)
        g.F[...]=s
        return jnp.sum(s*s,axis=0,keepdims=True)
    def drain(g):
        P=g.P
        for i in range(15):
            rcopy(g.view(P.chip),g.X.at[i],g.ss.at[i],g.rs.at[i],P.sib).wait_send()
        g.d0.wait_send()

class ReducePlane:
    def __init__(g,P,G,b,hc,rb,R,X,F,ss,rs):
        g.P,g.G,g.b,g.hc,g.rb,g.R,g.X,g.F,g.ss,g.rs=P,G,b,hc,rb,R,X,F,ss,rs
    def cs(g,h): return pl.ds(pl.multiple_of(h*g.hc,128),g.hc)
    def rs_(g,p,part=None,local=False):
        n=g.rb
        r0=(p-4*g.b if local else p)*n
        if part is not None: n=n//2; r0=r0+part*n
        return pl.ds(pl.multiple_of(r0,n),n)
    def start(g):
        P=g.P
        g.d0=rcopy(g.G.at[pl.ds(g.b*4*g.rb,4*g.rb),g.cs(1-P.c)],g.R,g.ss.at[15],g.rs.at[15],P.sib); g.d0.start()
    def view(g,p,part=None): return g.G.at[g.rs_(p,part),g.cs(g.P.c)]
    def xv(g,i,part=None):
        if part is None: return g.X.at[i]
        return g.X.at[i,pl.ds(part*(g.rb//2),g.rb//2)]
    def cp(g,p,i,sem,dev,part=None):
        return rcopy(g.view(p,part),g.xv(i,part),g.ss.at[sem],g.rs.at[sem],dev)
    def addR(g,p):
        a=g.G[g.rs_(p),g.cs(g.P.c)].astype(f32)+g.R[g.rs_(p,None,True),:].astype(f32)
        g.G[g.rs_(p),g.cs(g.P.c)]=a.astype(bf)
    def step_c(g):
        P=g.P; g.d0.wait_recv()
        pd=P.p(g.b,1,1); g.addR(pd)
        g.cp(pd,0,0,P.yn,0).start(); g.cp(pd,0,1,P.xn,1).start()
        for dy,dx in ((0,1),(1,0),(0,0)): g.addR(P.p(g.b,dy,dx))
    def step_d(g):
        P=g.P; h=g.rb//2
        for part,(p,sem,dev,i) in enumerate(((P.p(g.b,0,1),0,P.xn,1),(P.p(g.b,1,0),1,P.yn,2))):
            g.cp(p,0,sem,P.sib,part).wait_recv()
            a=g.G[g.rs_(p,part),g.cs(P.c)].astype(f32)+g.X[0,part*h:part*h+h].astype(f32)
            g.G[g.rs_(p,part),g.cs(P.c)]=a.astype(bf)
            g.cp(p,i,1+i,dev).start()
    def step_xy(g):
        P=g.P; p=P.p(g.b,0,0)
        g.cp(p,1,2,P.sib).wait_recv(); g.cp(p,2,3,P.sib).wait_recv()
        s=g.G[g.rs_(p),g.cs(P.c)].astype(f32)+g.X[1].astype(f32)+g.X[2].astype(f32)
        g.F[...]=s
        @pl.when(P.z!=g.b)
        def _():
            g.G[g.rs_(p),g.cs(P.c)]=s.astype(bf)
            k=(P.z+4-g.b)%4
            rcopy(g.view(p),g.X.at[2+k],g.ss.at[4],g.rs.at[3+k],P.zdev(g.b)).start()
    def step_z(g,FD):
        P=g.P; p=P.p(g.b,0,0)
        @pl.when(P.z==g.b)
        def _():
            s=g.F[...]
            for k in (1,2,3):
                v=g.X.at[2+k]; rcopy(v,v,g.ss.at[4],g.rs.at[3+k],P.sib).wait_recv()
                s=s+g.X[2+k].astype(f32)
            FD[...]=s
    def drain(g):
        P=g.P; p=P.chip
        g.cp(p,0,0,P.sib,0).wait_send(); g.cp(p,0,1,P.sib,1).wait_send()
        g.cp(p,1,2,P.sib).wait_send(); g.cp(p,2,3,P.sib).wait_send()
        @pl.when(P.z!=g.b)
        def _(): g.cp(p,1,4,P.sib).wait_send()
        g.d0.wait_send()

HBM=pl.BlockSpec(memory_space=pl.ANY)

def gather_kernel(wi,wo,wu,wd,oi,oo,ou,od,Wi,Wo,Wu,Wd,Xi,Xo,Xu,Xd,ss,rs,es,er,ls,os_):
    P=Place()
    entry_barrier(P)
    pre=[]
    for i,(s,X) in enumerate(((wi,Xi),(wo,Xo),(wu,Xu),(wd,Xd))):
        dst=X.at[P.c]
        if i==0: dst=X.at[P.c,:,pl.ds(0,WIN)]
        r=rcopy(s,dst,es.at[i],er.at[i],P.sib); r.start()
        l=pltpu.make_async_copy(s,dst,ls.at[i]); l.start()
        pre.append((r,l))
    def pack(i,X,W,n,cols,hc):
        r,l=pre[i]; r.wait(); l.wait()
        for h in range(1):
            v=jnp.concatenate([X[0,:,cols],X[1,:,cols]],axis=0).astype(bf)
            W[pl.ds(pl.multiple_of(P.chip*n,n),n),cols]=v
    Xi[:,:,1920:]=jnp.zeros((2,24,128),f32)
    c=P.c
    def cc(hc,o=0): return pl.ds(pl.multiple_of(o+c*hc,128),hc)
    pack(0,Xi,Wi,48,cc(1024),1024)
    items=[Gather(P,Wi,0,1024,48,ss.at[0],rs.at[0])]
    items[0].start()
    pack(1,Xo,Wo,48,cc(384),384)
    items.append(Gather(P,Wo,0,384,48,ss.at[1],rs.at[1])); items[1].start()
    for b in range(4):
        if b==0:
            r,l=pre[2]; r.wait(); l.wait()
            r,l=pre[3]; r.wait(); l.wait()
            W=Wd; cols=cc(384)
            W[pl.ds(pl.multiple_of(P.chip*192,192),192),cols]=jnp.concatenate([Xd[0,:,cols],Xd[1,:,cols]],axis=0).astype(bf)
        cols=cc(384,768*b)
        Wu[pl.ds(pl.multiple_of(P.chip*48,48),48),cols]=jnp.concatenate([Xu[0,:,cols],Xu[1,:,cols]],axis=0).astype(bf)
        g=Gather(P,Wu,768*b,384,48,ss.at[2+2*b],rs.at[2+2*b]); g.start(); items.append(g)
        g=GatherPlane(P,Wd,b,384,192,ss.at[3+2*b],rs.at[3+2*b]); g.start(); items.append(g)
    stages=["step_z","step_xy","step_d","finish"]
    n=len(items)
    for t in range(n+len(stages)-1):
        for s in reversed(range(len(stages))):
            i=t-s
            if 0<=i<n: getattr(items[i],stages[s])()
    for g in items: g.drain()
    cps=[]
    for i,(a,b) in enumerate(((Wi,oi),(Wo,oo),(Wu,ou),(Wd,od))):
        cp=pltpu.make_async_copy(a,b,os_.at[i]); cp.start(); cps.append(cp)
    for cp in cps: cp.wait()

def gather_weights(wi,wo,wu,wd):
    V=pltpu.VMEM; S=pltpu.SemaphoreType.DMA
    sh=lambda s: jax.ShapeDtypeStruct(s,bf)
    return pl.pallas_call(gather_kernel,out_shape=[sh((D,WPAD)),sh((D,D)),sh((D,FF)),sh((FF,D))],
      in_specs=[HBM]*4,out_specs=[HBM]*4,
      scratch_shapes=[V((D,WPAD),bf),V((D,D),bf),V((D,FF),bf),V((FF,D),bf),V((2,24,WPAD),f32),V((2,24,D),f32),V((2,24,FF),f32),V((2,96,D),f32),
        S((10,16)),S((10,16)),S((4,)),S((4,)),S((4,)),S((4,))],
      compiler_params=pltpu.CompilerParams(collective_id=1,has_side_effects=True,vmem_limit_bytes=60<<20))(wi,wo,wu,wd)

def reduce_kernel(gi,go,gu,gd,oi,oo,ou,od,sq,Gi,Go,Gu,Gd,Ri,Ro,Ru,Rd,Xi,Xo,Xu,Xd,Fi,Fo,Fu,Fp,Fd,ss,rs,ls,es,er,fs):
    P=Place()
    entry_barrier(P)
    cps=[]
    for i,(a,b) in enumerate(((gi,Gi),(go,Go),(gu,Gu),(gd,Gd))):
        cp=pltpu.make_async_copy(a,b,ls.at[i]); cp.start(); cps.append(cp)
    for cp in cps: cp.wait()
    items=[]
    for b in range(4):
        items.append(Reduce(P,Gu,768*b,384,48,Ru.at[b],Xu.at[b],Fu.at[b],ss.at[2+2*b],rs.at[2+2*b]))
        items.append(ReducePlane(P,Gd,b,384,192,Rd.at[b],Xd.at[b],Fp.at[b],ss.at[3+2*b],rs.at[3+2*b]))
    items.append(Reduce(P,Go,0,384,48,Ro,Xo,Fo,ss.at[1],rs.at[1]))
    items.append(Reduce(P,Gi,0,1024,48,Ri,Xi,Fi,ss.at[0],rs.at[0]))
    tot=[]
    def last(g):
        if isinstance(g,ReducePlane): g.step_z(Fd)
        else: tot.append(jnp.sum(g.step_z(),axis=1,keepdims=True))
    stages=["start","step_c","step_d","step_xy",None]
    n=len(items)
    for t in range(n+len(stages)-1):
        for s in reversed(range(len(stages))):
            i=t-s
            if 0<=i<n:
                if s==4: last(items[i])
                else: getattr(items[i],stages[s])()
    tot.append(jnp.sum(jnp.sum(Fd[...]*Fd[...],axis=0,keepdims=True),axis=1,keepdims=True))
    sq[...]=jnp.broadcast_to(sum(tot),(8,128))
    c=P.c; fin=[]
    e=0
    for F,O,c0,hc,n in [(Fi,oi,0,1024,24),(Fo,oo,0,384,24)]+[(Fu.at[b],ou,768*b,384,24) for b in range(4)]+[(Fd,od,0,384,96)]:
        cols=pl.ds(pl.multiple_of(c0+c*hc,128),hc)
        r=rcopy(F.at[pl.ds(pl.multiple_of((1-c)*n,8),n)],O.at[:,cols],es.at[e],er.at[e],P.sib); r.start()
        l=pltpu.make_async_copy(F.at[pl.ds(pl.multiple_of(c*n,8),n)],O.at[:,cols],fs.at[e]); l.start()
        fin+= [r,l]; e+=1
    for f in fin: f.wait()
    for g in items: g.drain()

def reduce_grads(gi,go,gu,gd):
    V=pltpu.VMEM; S=pltpu.SemaphoreType.DMA
    sh=lambda s: jax.ShapeDtypeStruct(s,f32)
    return pl.pallas_call(reduce_kernel,out_shape=[sh((24,WPAD)),sh((24,D)),sh((24,FF)),sh((96,D)),sh((8,128))],
      in_specs=[HBM]*4,out_specs=[HBM]*4+[pl.BlockSpec(memory_space=pltpu.VMEM)],
      scratch_shapes=[V((D,WPAD),bf),V((D,D),bf),V((D,FF),bf),V((FF,D),bf),
        V((D,1024),bf),V((D,384),bf),V((4,D,384),bf),V((4,D,384),bf),
        V((15,48,1024),bf),V((15,48,384),bf),V((4,15,48,384),bf),V((4,6,192,384),bf),
        V((48,1024),f32),V((48,384),f32),V((4,48,384),f32),V((4,192,384),f32),V((192,384),f32),
        S((10,16)),S((10,16)),S((4,)),S((7,)),S((7,)),S((7,))],
      compiler_params=pltpu.CompilerParams(collective_id=2,has_side_effects=True,vmem_limit_bytes=60<<20))(gi,go,gu,gd)
D = 768
H = 12
HD = 64
FF = 3072
VH = 6
STEP = 7


BETA_ONE = 0.5
BETA_TWO = 0.5
SHADOW_RATE = 0.5
RATE_MATRIX = 0.03
RATE_OUTPUT = 0.15
RATE_VECTOR = 0.3
DECAY_MATRIX = 0.1
CLIP = 1.0
EPS_ADAM = 1e-08
SCORE_SCALE = 0.125


def norm_rows(values, gain, shift):
    center = values - jnp.mean(values, axis=-1, keepdims=True)
    spread = jnp.mean(center * center, axis=-1, keepdims=True)
    return center * lax.rsqrt(spread + 1e-05) * gain + shift


def split_vector(vector):
    extents = [D, D, D, D, H * HD, VH * HD, D, FF, D]
    pieces = []
    offset = 0
    for extent in extents:
        pieces.append(vector[offset : offset + extent])
        offset += extent
    return pieces


def gather_copies(lowered):
    return (
        lax.all_gather(lowered[0], ("wide", "narrow"), axis=0, tiled=True),
        lax.all_gather(lowered[1], ("wide", "narrow"), axis=0, tiled=True),
        lax.all_gather(lowered[2], ("wide", "narrow"), axis=0, tiled=True),
        lax.all_gather(lowered[3], ("wide", "narrow"), axis=0, tiled=True),
    )


def sum_gradients(partials):
    return (
        lax.psum_scatter(partials[0], ("wide", "narrow"), scatter_dimension=0, tiled=True),
        lax.psum_scatter(partials[1], ("wide", "narrow"), scatter_dimension=0, tiled=True),
        lax.psum_scatter(partials[2], ("wide", "narrow"), scatter_dimension=0, tiled=True),
        lax.psum_scatter(partials[3], ("wide", "narrow"), scatter_dimension=0, tiled=True),
    )


def adam_step(master, grad, first, second, shadow, rate, decay):
    moment = BETA_ONE * first + (1.0 - BETA_ONE) * grad
    square = BETA_TWO * second + (1.0 - BETA_TWO) * grad * grad
    moment_hat = moment / (1.0 - BETA_ONE**STEP)
    square_hat = square / (1.0 - BETA_TWO**STEP)
    updated = master - rate * (moment_hat / (jnp.sqrt(square_hat) + EPS_ADAM) + decay * master)
    average = SHADOW_RATE * shadow + (1.0 - SHADOW_RATE) * updated
    return (updated, moment, square, average)


def body(
    tokens,
    first_values,
    cotangent,
    lengths,
    weight_in,
    weight_out,
    weight_up,
    weight_down,
    first_in,
    first_out,
    first_up,
    first_down,
    second_in,
    second_out,
    second_up,
    second_down,
    shadow_in,
    shadow_out,
    shadow_up,
    shadow_down,
    vectors,
    first_vectors,
    second_vectors,
    shadow_vectors,
):
    masters = (weight_in, weight_out, weight_up, weight_down)
    lowered = tuple((master.astype(jnp.bfloat16) for master in masters))
    custom = MESH_SIZES == (8, 4)
    if custom:
        gathered = gather_weights(*masters)
        copies = (gathered[0][:, :WIN],) + tuple(gathered[1:])
    else:
        copies = gather_copies(lowered)
    slot_count, seq_len = (tokens.shape[0], tokens.shape[1])
    row_count = slot_count * seq_len
    span = H * HD
    (
        gain_one,
        shift_one,
        gain_two,
        shift_two,
        bias_query,
        bias_value,
        bias_out,
        bias_up,
        bias_down,
    ) = split_vector(vectors)
    positions = jnp.arange(seq_len, dtype=jnp.int32)
    valid = (positions[None, :] < lengths[:, None]).astype(jnp.float32).reshape(row_count, 1)
    inputs = tokens.astype(jnp.float32).reshape(row_count, D)
    normed = norm_rows(inputs, gain_one, shift_one)
    normed_low = normed.astype(jnp.bfloat16)
    project = jnp.dot(normed_low, copies[0], preferred_element_type=jnp.float32)
    query_low = (project[:, :span] + bias_query).astype(jnp.bfloat16)
    key_low = project[:, span : 2 * span].astype(jnp.bfloat16)
    fresh_low = (project[:, 2 * span :] + bias_value).astype(jnp.bfloat16)
    query_heads = query_low.reshape(slot_count, seq_len, H, HD)
    key_heads = key_low.reshape(slot_count, seq_len, H, HD)
    value_heads = jnp.concatenate(
        [
            fresh_low.reshape(slot_count, seq_len, VH, HD),
            first_values.reshape(slot_count, seq_len, H - VH, HD),
        ],
        axis=2,
    )
    block = min(512, seq_len)
    per_slot = seq_len // block
    block_ids = jnp.arange(slot_count * per_slot, dtype=jnp.int32)

    def masked_scores(index):
        slot = index // per_slot
        offset = index % per_slot * block
        query_block = lax.dynamic_slice_in_dim(
            lax.dynamic_index_in_dim(query_heads, slot, 0, False), offset, block, 0
        )
        key_slot = lax.dynamic_index_in_dim(key_heads, slot, 0, False)
        value_slot = lax.dynamic_index_in_dim(value_heads, slot, 0, False)
        raw = (
            jnp.einsum("qhe,khe->hqk", query_block, key_slot, preferred_element_type=jnp.float32)
            * SCORE_SCALE
        )
        row_pos = offset + jnp.arange(block, dtype=jnp.int32)
        column_pos = jnp.arange(seq_len, dtype=jnp.int32)
        length = lax.dynamic_index_in_dim(lengths, slot, 0, False)
        allowed = (column_pos[None, :] <= row_pos[:, None]) & (column_pos[None, :] < length)
        return (
            jnp.where(allowed[None], raw, -1000000000.0),
            slot,
            offset,
            query_block,
            key_slot,
            value_slot,
        )

    def forward_block(index):
        scores, slot, offset, query_block, key_slot, value_slot = masked_scores(index)
        highest = jnp.max(scores, axis=-1, keepdims=True)
        exponent = jnp.exp(scores - highest)
        summed = jnp.sum(exponent, axis=-1, keepdims=True)
        probs_low = (exponent / summed).astype(jnp.bfloat16)
        block_out = jnp.einsum(
            "hqk,khe->qhe", probs_low, value_slot, preferred_element_type=jnp.float32
        )
        return (block_out, (highest + jnp.log(summed))[..., 0])

    attended, log_totals = lax.map(forward_block, block_ids)
    attended_low = attended.reshape(row_count, span).astype(jnp.bfloat16)
    branch = jnp.dot(attended_low, copies[1], preferred_element_type=jnp.float32) + bias_out
    middle = inputs + branch
    normed_two = norm_rows(middle, gain_two, shift_two)
    normed_two_low = normed_two.astype(jnp.bfloat16)
    hidden_pre = jnp.dot(normed_two_low, copies[2], preferred_element_type=jnp.float32) + bias_up
    active_low = jax.nn.gelu(hidden_pre, approximate=True).astype(jnp.bfloat16)
    feed = jnp.dot(active_low, copies[3], preferred_element_type=jnp.float32) + bias_down
    result = (valid * (middle + feed)).astype(jnp.bfloat16).reshape(slot_count, seq_len, D)
    back_copies = copies
    grad_out = cotangent.astype(jnp.float32).reshape(row_count, D) * valid
    grad_out_low = grad_out.astype(jnp.bfloat16)
    grad_down = jnp.einsum(
        "nf,nd->fd", active_low, grad_out_low, preferred_element_type=jnp.float32
    )
    grad_bias_down = jnp.sum(grad_out, axis=0)
    grad_active = jnp.einsum(
        "nd,fd->nf", grad_out_low, back_copies[3], preferred_element_type=jnp.float32
    )
    unused, gelu_back = jax.vjp(lambda values: jax.nn.gelu(values, approximate=True), hidden_pre)
    grad_hidden_low = gelu_back(grad_active)[0].astype(jnp.bfloat16)
    grad_up = jnp.einsum(
        "nd,nf->df", normed_two_low, grad_hidden_low, preferred_element_type=jnp.float32
    )
    grad_bias_up = jnp.sum(grad_hidden_low.astype(jnp.float32), axis=0)
    grad_normed_two = jnp.einsum(
        "nf,df->nd", grad_hidden_low, back_copies[2], preferred_element_type=jnp.float32
    )
    unused, norm_two_back = jax.vjp(norm_rows, middle, gain_two, shift_two)
    grad_middle_norm, grad_gain_two, grad_shift_two = norm_two_back(grad_normed_two)
    grad_middle = grad_out + grad_middle_norm
    grad_branch_low = grad_middle.astype(jnp.bfloat16)
    grad_weight_out = jnp.einsum(
        "ne,nd->ed", attended_low, grad_branch_low, preferred_element_type=jnp.float32
    )
    grad_bias_out = jnp.sum(grad_branch_low.astype(jnp.float32), axis=0)
    grad_attended_low = jnp.einsum(
        "nd,ed->ne", grad_branch_low, back_copies[1], preferred_element_type=jnp.float32
    ).astype(jnp.bfloat16)
    grad_heads = grad_attended_low.reshape(slot_count, seq_len, H, HD)

    def backward_block(index):
        scores, slot, offset, query_block, key_slot, value_slot = masked_scores(index)
        grad_block = lax.dynamic_slice_in_dim(
            lax.dynamic_index_in_dim(grad_heads, slot, 0, False), offset, block, 0
        )
        log_block = lax.dynamic_index_in_dim(log_totals, index, 0, False)
        probs = jnp.exp(scores - log_block[..., None])
        probs_low = probs.astype(jnp.bfloat16)
        grad_probs = jnp.einsum(
            "qhe,khe->hqk", grad_block, value_slot, preferred_element_type=jnp.float32
        )
        inner = jnp.sum(probs * grad_probs, axis=-1, keepdims=True)
        grad_scores = (probs * (grad_probs - inner)).astype(jnp.bfloat16)
        grad_query = (
            jnp.einsum("hqk,khe->qhe", grad_scores, key_slot, preferred_element_type=jnp.float32)
            * SCORE_SCALE
        )
        grad_key = (
            jnp.einsum("hqk,qhe->khe", grad_scores, query_block, preferred_element_type=jnp.float32)
            * SCORE_SCALE
        )
        grad_value = jnp.einsum(
            "hqk,qhe->khe", probs_low, grad_block, preferred_element_type=jnp.float32
        )
        return (grad_query, grad_key, grad_value)

    grad_query, grad_key, grad_value = lax.map(backward_block, block_ids)
    grad_query_low = grad_query.reshape(row_count, span).astype(jnp.bfloat16)
    grad_key_low = (
        grad_key.reshape(slot_count, per_slot, seq_len, H, HD)
        .sum(axis=1)
        .reshape(row_count, span)
        .astype(jnp.bfloat16)
    )
    grad_value_all = grad_value.reshape(slot_count, per_slot, seq_len, H, HD).sum(axis=1)
    grad_fresh_low = grad_value_all[:, :, :VH].reshape(row_count, VH * HD).astype(jnp.bfloat16)
    grad_values = (
        grad_value_all[:, :, VH:].reshape(slot_count, seq_len, (H - VH) * HD).astype(jnp.bfloat16)
    )
    grad_bias_query = jnp.sum(grad_query_low.astype(jnp.float32), axis=0)
    grad_bias_value = jnp.sum(grad_fresh_low.astype(jnp.float32), axis=0)
    grad_project = jnp.concatenate([grad_query_low, grad_key_low, grad_fresh_low], axis=1)
    grad_weight_in = jnp.einsum(
        "nd,ne->de", normed_low, grad_project, preferred_element_type=jnp.float32
    )
    grad_normed = jnp.einsum(
        "ne,de->nd", grad_project, back_copies[0], preferred_element_type=jnp.float32
    )
    unused, norm_one_back = jax.vjp(norm_rows, inputs, gain_one, shift_one)
    grad_inputs_norm, grad_gain_one, grad_shift_one = norm_one_back(grad_normed)
    grad_tokens = (
        (grad_middle + grad_inputs_norm).astype(jnp.bfloat16).reshape(slot_count, seq_len, D)
    )
    if custom:
        low = tuple(g.astype(jnp.bfloat16) for g in (grad_weight_in, grad_weight_out, grad_up, grad_down))
        padded = jnp.pad(low[0], ((0, 0), (0, WPAD - WIN)))
        *shards, squares = reduce_grads(padded, *low[1:])
        shards[0] = shards[0][:, :WIN]
    else:
        shards = sum_gradients((grad_weight_in, grad_weight_out, grad_up, grad_down))
    local_squares = jnp.float32(0.0)
    for shard in shards:
        local_squares = local_squares + jnp.sum(shard * shard)
    vector_partial = jnp.concatenate(
        [
            grad_gain_one,
            grad_shift_one,
            grad_gain_two,
            grad_shift_two,
            grad_bias_query,
            grad_bias_value,
            grad_bias_out,
            grad_bias_up,
            grad_bias_down,
        ]
    )
    vector_grad, matrix_squares = lax.psum((vector_partial, local_squares), ("wide", "narrow"))
    grad_norm = jnp.sqrt(matrix_squares + jnp.sum(vector_grad * vector_grad))
    factor = jnp.minimum(1.0, CLIP / grad_norm)
    firsts = (first_in, first_out, first_up, first_down)
    seconds = (second_in, second_out, second_up, second_down)
    shadows = (shadow_in, shadow_out, shadow_up, shadow_down)
    rates = (RATE_MATRIX, RATE_OUTPUT, RATE_MATRIX, RATE_MATRIX)
    outputs = [result, grad_tokens, grad_values, grad_norm]
    for index in range(4):
        outputs.extend(
            adam_step(
                masters[index],
                factor * shards[index],
                firsts[index],
                seconds[index],
                shadows[index],
                rates[index],
                DECAY_MATRIX,
            )
        )
    outputs.extend(
        adam_step(
            vectors,
            factor * vector_grad,
            first_vectors,
            second_vectors,
            shadow_vectors,
            RATE_VECTOR,
            0.0,
        )
    )
    return tuple(outputs)


def solution(mesh):
    global MESH_SIZES
    MESH_SIZES = (mesh.shape["wide"], mesh.shape["narrow"])
    return jax.shard_map(
        body,
        mesh=mesh,
        in_specs=(
            P(("wide", "narrow"), None, None),
            P(("wide", "narrow"), None, None),
            P(("wide", "narrow"), None, None),
            P(("wide", "narrow")),
            P(("wide", "narrow"), None),
            P(("wide", "narrow"), None),
            P(("wide", "narrow"), None),
            P(("wide", "narrow"), None),
            P(("wide", "narrow"), None),
            P(("wide", "narrow"), None),
            P(("wide", "narrow"), None),
            P(("wide", "narrow"), None),
            P(("wide", "narrow"), None),
            P(("wide", "narrow"), None),
            P(("wide", "narrow"), None),
            P(("wide", "narrow"), None),
            P(("wide", "narrow"), None),
            P(("wide", "narrow"), None),
            P(("wide", "narrow"), None),
            P(("wide", "narrow"), None),
            P(),
            P(),
            P(),
            P(),
        ),
        out_specs=(
            P(("wide", "narrow"), None, None),
            P(("wide", "narrow"), None, None),
            P(("wide", "narrow"), None, None),
            P(),
            P(("wide", "narrow"), None),
            P(("wide", "narrow"), None),
            P(("wide", "narrow"), None),
            P(("wide", "narrow"), None),
            P(("wide", "narrow"), None),
            P(("wide", "narrow"), None),
            P(("wide", "narrow"), None),
            P(("wide", "narrow"), None),
            P(("wide", "narrow"), None),
            P(("wide", "narrow"), None),
            P(("wide", "narrow"), None),
            P(("wide", "narrow"), None),
            P(("wide", "narrow"), None),
            P(("wide", "narrow"), None),
            P(("wide", "narrow"), None),
            P(("wide", "narrow"), None),
            P(),
            P(),
            P(),
            P(),
        ),
        check_vma=False,
    )
```

```python
import functools

import jax
import jax.numpy as jnp
from jax import lax
from jax.experimental import pallas as pl
from jax.experimental.pallas import tpu as pltpu
from jax.sharding import PartitionSpec as P

D = 768
H = 12
HD = 64
FF = 3072
VH = 6
STEP = 7
BETA_ONE = 0.5
BETA_TWO = 0.5
SHADOW_RATE = 0.5
RATE_MATRIX = 0.03
RATE_OUTPUT = 0.15
RATE_VECTOR = 0.3
DECAY_MATRIX = 0.1
CLIP = 1.0
EPS_ADAM = 1e-08

bf = jnp.bfloat16
f32 = jnp.float32
MESH = pl.DeviceIdType.MESH
WIN = 2 * D + VH * HD
WPAD = 2048
FB = 768
NB = FF // FB
QB = 256
PAIR = 2 * HD
PAIRS = H // 2

OFF = {}
_at = 0
for _name, _n in (("g1", D), ("b1", D), ("g2", D), ("b2", D), ("bq", D), ("bv", VH * HD), ("bo", D), ("bu", FF), ("bd", D)):
    OFF[_name] = (_at, _n)
    _at += _n
VEC = _at
EARLY = ("g2", "b2", "bo", "bu", "bd")
LATE = ("g1", "b1", "bq", "bv")


def offsets_in(names):
    where, at = {}, 0
    for name in names:
        where[name] = at
        at += OFF[name][1]
    return where, at


EARLY_AT, EARLY_N = offsets_in(EARLY)
LATE_AT, LATE_N = offsets_in(LATE)
LATE_ALL = LATE_N + 128


def nn(a, b):
    return lax.dot_general(a, b, (((1,), (0,)), ((), ())), preferred_element_type=f32)


def nt(a, b):
    return lax.dot_general(a, b, (((1,), (1,)), ((), ())), preferred_element_type=f32)


def tn(a, b):
    return lax.dot_general(a, b, (((0,), (0,)), ((), ())), preferred_element_type=f32)


def blk(i, n):
    return pl.ds(i * n if isinstance(i, int) else pl.multiple_of(i * n, n), n)


def lanes(start, n):
    return pl.ds(start if isinstance(start, int) else pl.multiple_of(start, 128), n)


def colsum(v):
    return jnp.sum(v, axis=0, keepdims=True)


class Place:
    def __init__(s):
        s.w = lax.axis_index("wide")
        s.n = lax.axis_index("narrow")
        s.z, s.y, s.x, s.c = s.w // 2, s.w % 2, s.n // 2, s.n % 2
        s.sib = (s.w, s.n + 1 - 2 * s.c)
        s.xn = (s.w, (s.n + 2) % 4)
        s.yn = (s.w + 1 - 2 * s.y, s.n)
        s.chip = s.z * 4 + s.y * 2 + s.x

    def zdev(s, zt):
        return (zt * 2 + s.y, s.n)

    def p(s, zt, dy, dx):
        yy = 1 - s.y if dy else s.y
        xx = 1 - s.x if dx else s.x
        return zt * 4 + yy * 2 + xx


def rcopy(src, dst, ss, rs, dev):
    return pltpu.make_async_remote_copy(
        src_ref=src, dst_ref=dst, send_sem=ss, recv_sem=rs, device_id=dev, device_id_type=MESH
    )


def entry_barrier(at):
    bar = pltpu.get_barrier_semaphore()
    for k in (1, 2, 3):
        pl.semaphore_signal(bar, inc=1, device_id=(at.w, (at.n + k) % 4), device_id_type=MESH)
    for k in range(1, 8):
        pl.semaphore_signal(bar, inc=1, device_id=((at.w + k) % 8, at.n), device_id_type=MESH)
    pl.semaphore_wait(bar, 10)


class Gather:
    def __init__(g, at, W, col0, stride, hc, rb, ss, rs, bulk):
        g.bulk = bulk
        g.at, g.W, g.col0, g.stride, g.hc, g.rb, g.ss, g.rs = at, W, col0, stride, hc, rb, ss, rs

    def cols(g, h):
        return lanes(g.col0 + h * g.stride, g.hc)

    def view(g, p):
        return g.W.at[blk(p, g.rb), g.cols(g.at.c)]

    def half(g, h):
        return g.W.at[:, g.cols(h)]

    def put(g, p, i, dev):
        if i == 15 and g.bulk:
            return
        v = g.view(p)
        rcopy(v, v, g.ss.at[i], g.rs.at[i], dev).start()

    def share(g):
        v = g.half(g.at.c)
        rcopy(v, v, g.ss.at[15], g.rs.at[15], g.at.sib).start()

    def got(g, p, i):
        v = g.view(p)
        rcopy(v, v, g.ss.at[i], g.rs.at[i], g.at.sib).wait_recv()

    def zk(g, k):
        return (g.at.z + 4 - k) % 4

    def spread(g, p, k):
        g.put(p, 3 + k, g.at.xn)
        g.put(p, 9 + k, g.at.yn)
        g.put(p, 15, g.at.sib)

    def start(g):
        p = g.at.chip
        for k in (1, 2, 3):
            g.put(p, k - 1, g.at.zdev((g.at.z + k) % 4))
        g.spread(p, 0)

    def step_z(g, k):
        p = g.at.p(g.zk(k), 0, 0)
        g.got(p, k - 1)
        g.spread(p, k)

    def step_x(g, k):
        p = g.at.p(g.zk(k), 0, 1)
        g.got(p, 3 + k)
        if k < 2:
            g.put(p, 13 + k, g.at.yn)
        g.put(p, 15, g.at.sib)

    def step_y(g, k):
        p = g.at.p(g.zk(k), 1, 0)
        g.got(p, 9 + k)
        if k >= 2:
            g.put(p, 5 + k, g.at.xn)
        g.put(p, 15, g.at.sib)

    def step_d(g, k):
        p = g.at.p(g.zk(k), 1, 1)
        g.got(p, 13 + k if k < 2 else 5 + k)
        g.put(p, 15, g.at.sib)

    def finish(g):
        v = g.half(1 - g.at.c)
        rcopy(v, v, g.ss.at[15], g.rs.at[15], g.at.sib).wait_recv()

    def drain(g):
        v = g.view(g.at.chip)
        for i in range(15):
            rcopy(v, v, g.ss.at[i], g.rs.at[i], g.at.sib).wait_send()
        v = g.half(g.at.c)
        rcopy(v, v, g.ss.at[15], g.rs.at[15], g.at.sib).wait_send()


class GatherPlane:
    def __init__(g, at, W, b, hc, rb, ss, rs):
        g.bulk = True
        g.at, g.W, g.b, g.hc, g.rb, g.ss, g.rs = at, W, b, hc, rb, ss, rs

    def view(g, p, part=None):
        n = g.rb if part is None else g.rb // 2
        r0 = p * g.rb if part is None else p * g.rb + part * n
        return g.W.at[pl.ds(pl.multiple_of(r0, n), n), lanes(g.at.c * g.hc, g.hc)]

    def half(g, h):
        return g.W.at[pl.ds(g.b * 4 * g.rb, 4 * g.rb), lanes(h * g.hc, g.hc)]

    def share(g):
        v = g.half(g.at.c)
        rcopy(v, v, g.ss.at[15], g.rs.at[15], g.at.sib).start()

    def put(g, p, i, dev, part=None):
        if i == 15:
            return
        v = g.view(p, part)
        rcopy(v, v, g.ss.at[i], g.rs.at[i], dev).start()

    def got(g, p, i, part=None):
        v = g.view(p, part)
        rcopy(v, v, g.ss.at[i], g.rs.at[i], g.at.sib).wait_recv()

    def start(g):
        at = g.at

        @pl.when(at.z == g.b)
        def _():
            for k in (1, 2, 3):
                g.put(at.chip, k - 1, at.zdev((at.z + k) % 4))

    def step_z(g):
        at = g.at
        p = at.p(g.b, 0, 0)

        @pl.when(at.z != g.b)
        def _():
            k = (at.z + 4 - g.b) % 4
            v = g.view(p)
            rcopy(v, v, g.ss.at[k - 1], g.rs.at[k - 1], at.sib).wait_recv()

        g.put(p, 3, at.xn)
        g.put(p, 4, at.yn)
        g.put(p, 15, at.sib)

    def step_x(g):
        p = g.at.p(g.b, 0, 1)
        g.got(p, 3)
        g.put(p, 5, g.at.yn, 0)
        g.put(p, 15, g.at.sib)

    def step_y(g):
        p = g.at.p(g.b, 1, 0)
        g.got(p, 4)
        g.put(p, 6, g.at.xn, 1)
        g.put(p, 15, g.at.sib)

    def step_d(g):
        pd = g.at.p(g.b, 1, 1)
        g.got(pd, 5, 0)
        g.got(pd, 6, 1)
        g.put(pd, 15, g.at.sib)

    def finish(g):
        v = g.half(1 - g.at.c)
        rcopy(v, v, g.ss.at[15], g.rs.at[15], g.at.sib).wait_recv()

    def drain(g):
        at = g.at
        v = g.view(at.chip)

        @pl.when(at.z == g.b)
        def _():
            for i in range(3):
                rcopy(v, v, g.ss.at[i], g.rs.at[i], at.sib).wait_send()

        for i in (3, 4):
            rcopy(v, v, g.ss.at[i], g.rs.at[i], at.sib).wait_send()
        v = g.view(at.chip, 0)
        for i in (5, 6):
            rcopy(v, v, g.ss.at[i], g.rs.at[i], at.sib).wait_send()
        v = g.half(at.c)
        rcopy(v, v, g.ss.at[15], g.rs.at[15], at.sib).wait_send()


class Reduce:
    def __init__(g, at, G, col0, stride, hc, rb, R, X, F, ss, rs):
        g.at, g.G, g.col0, g.stride, g.hc, g.rb = at, G, col0, stride, hc, rb
        g.R, g.X, g.F, g.ss, g.rs = R, X, F, ss, rs

    def cols(g, h):
        return lanes(g.col0 + h * g.stride, g.hc)

    def mine(g):
        return g.cols(g.at.c)

    def view(g, p):
        return g.G.at[blk(p, g.rb), g.mine()]

    def load(g, p):
        return g.G[blk(p, g.rb), g.mine()].astype(f32)

    def store(g, p, v):
        g.G[blk(p, g.rb), g.mine()] = v.astype(bf)

    def first(g):
        return rcopy(g.G.at[:, g.cols(1 - g.at.c)], g.R, g.ss.at[15], g.rs.at[15], g.at.sib)

    def start(g):
        g.first().start()

    def put(g, p, i, dev):
        rcopy(g.view(p), g.X.at[i], g.ss.at[i], g.rs.at[i], dev).start()

    def got(g, i):
        v = g.X.at[i]
        rcopy(v, v, g.ss.at[i], g.rs.at[i], g.at.sib).wait_recv()

    def add_core(g, p):
        g.store(p, g.load(p) + g.R[blk(p, g.rb), :].astype(f32))

    def step_c(g):
        at = g.at
        g.first().wait_recv()
        for zt in range(4):
            p = at.p(zt, 1, 1)
            g.add_core(p)
            g.put(p, zt, at.yn if zt < 2 else at.xn)
        for zt in range(4):
            p = at.p(zt, 1, 0) if zt < 2 else at.p(zt, 0, 1)
            g.add_core(p)
            if zt < 2:
                g.put(p, 8 + zt, at.yn)
            else:
                g.put(p, 4 + zt, at.xn)

    def step_d(g, zt):
        at = g.at
        p = at.p(zt, 0, 1) if zt < 2 else at.p(zt, 1, 0)
        g.got(zt)
        g.store(p, g.load(p) + (g.R[blk(p, g.rb), :].astype(f32) + g.X[zt].astype(f32)))
        if zt < 2:
            g.put(p, 4 + zt, at.xn)
        else:
            g.put(p, 8 + zt, at.yn)

    def step_xy(g, k):
        at = g.at
        zt = (at.z + k) % 4
        g.got(4 + zt)
        g.got(8 + zt)
        p = at.p(zt, 0, 0)
        s = g.load(p) + g.R[blk(p, g.rb), :].astype(f32)
        s = s + (g.X[4 + zt].astype(f32) + g.X[8 + zt].astype(f32))
        if k:
            g.store(p, s)
            g.put(p, 11 + k, at.zdev(zt))
        else:
            g.F[...] = s

    def step_z(g):
        s = g.F[...]
        for k in (1, 2, 3):
            g.got(11 + k)
            s = s + g.X[11 + k].astype(f32)
        g.F[...] = s

    def drain(g):
        for i in range(15):
            rcopy(g.view(g.at.chip), g.X.at[i], g.ss.at[i], g.rs.at[i], g.at.sib).wait_send()
        g.first().wait_send()


class ReducePlane:
    def __init__(g, at, G, b, hc, rb, R, X, F, ss, rs):
        g.at, g.G, g.b, g.hc, g.rb, g.R, g.X, g.F, g.ss, g.rs = at, G, b, hc, rb, R, X, F, ss, rs

    def cols(g, h):
        return lanes(h * g.hc, g.hc)

    def span(g, p, part=None, local=False):
        n = g.rb
        r0 = (p - 4 * g.b) * n if local else p * n
        if part is not None:
            n = n // 2
            r0 = r0 + part * n
        return pl.ds(pl.multiple_of(r0, n), n)

    def first(g):
        src = g.G.at[pl.ds(g.b * 4 * g.rb, 4 * g.rb), g.cols(1 - g.at.c)]
        return rcopy(src, g.R, g.ss.at[15], g.rs.at[15], g.at.sib)

    def start(g):
        g.first().start()

    def copy(g, p, i, slot, dev, part=None):
        src = g.G.at[g.span(p, part), g.cols(g.at.c)]
        dst = g.X.at[i]
        if part is not None:
            dst = g.X.at[i, pl.ds(part * (g.rb // 2), g.rb // 2)]
        return rcopy(src, dst, g.ss.at[slot], g.rs.at[slot], dev)

    def load(g, p, part=None):
        return g.G[g.span(p, part), g.cols(g.at.c)].astype(f32)

    def store(g, p, v, part=None):
        g.G[g.span(p, part), g.cols(g.at.c)] = v.astype(bf)

    def add_core(g, p):
        g.store(p, g.load(p) + g.R[g.span(p, None, True), :].astype(f32))

    def step_c(g):
        at = g.at
        g.first().wait_recv()
        pd = at.p(g.b, 1, 1)
        g.add_core(pd)
        g.copy(pd, 0, 0, at.yn, 0).start()
        g.copy(pd, 0, 1, at.xn, 1).start()
        g.add_core(at.p(g.b, 0, 1))
        g.add_core(at.p(g.b, 1, 0))

    def step_d(g):
        at = g.at
        h = g.rb // 2
        for part, p, slot, dev, i in ((0, at.p(g.b, 0, 1), 0, at.xn, 1), (1, at.p(g.b, 1, 0), 1, at.yn, 2)):
            g.copy(p, 0, slot, at.sib, part).wait_recv()
            g.store(p, g.load(p, part) + g.X[0, part * h : part * h + h].astype(f32), part)
            g.copy(p, i, 1 + i, dev).start()

    def step_xy(g):
        at = g.at
        p = at.p(g.b, 0, 0)
        g.copy(p, 1, 2, at.sib).wait_recv()
        g.copy(p, 2, 3, at.sib).wait_recv()
        s = g.load(p) + g.R[g.span(p, None, True), :].astype(f32)
        s = s + (g.X[1].astype(f32) + g.X[2].astype(f32))

        @pl.when(at.z == g.b)
        def _():
            g.F[...] = s

        @pl.when(at.z != g.b)
        def _():
            g.store(p, s)
            k = (at.z + 4 - g.b) % 4
            src = g.G.at[g.span(p), g.cols(at.c)]
            rcopy(src, g.X.at[2 + k], g.ss.at[4], g.rs.at[3 + k], at.zdev(g.b)).start()

    def step_z(g):
        at = g.at

        @pl.when(at.z == g.b)
        def _():
            s = g.F[...]
            for k in (1, 2, 3):
                v = g.X.at[2 + k]
                rcopy(v, v, g.ss.at[4], g.rs.at[3 + k], at.sib).wait_recv()
                s = s + g.X[2 + k].astype(f32)
            g.F[...] = s

    def drain(g):
        at = g.at
        p = at.chip
        g.copy(p, 0, 0, at.sib, 0).wait_send()
        g.copy(p, 0, 1, at.sib, 1).wait_send()
        g.copy(p, 1, 2, at.sib).wait_send()
        g.copy(p, 2, 3, at.sib).wait_send()

        @pl.when(at.z != g.b)
        def _():
            g.copy(p, 1, 4, at.sib).wait_send()

        g.first().wait_send()


class SumAll:
    def __init__(g, at, S, B, ss, rs):
        g.at, g.S, g.B, g.ss, g.rs = at, S, B, ss, rs

    def start(g):
        n = g.at.n
        for k in (1, 2, 3):
            rcopy(g.S.at[0], g.B.at[n], g.ss.at[k], g.rs.at[k], (g.at.w, (n + k) % 4)).start()
        g.B[n] = g.S[0]

    def middle(g):
        w, n = g.at.w, g.at.n
        for k in (1, 2, 3):
            v = g.B.at[(n + 4 - k) % 4]
            rcopy(v, v, g.ss.at[k], g.rs.at[k], g.at.sib).wait_recv()
        total = (g.B[0] + g.B[1]) + (g.B[2] + g.B[3])
        g.S[1] = total
        for k in range(1, 8):
            rcopy(g.S.at[1], g.B.at[4 + w], g.ss.at[3 + k], g.rs.at[3 + k], ((w + k) % 8, n)).start()
        g.B[4 + w] = total

    def last(g):
        w = g.at.w
        for k in range(1, 8):
            v = g.B.at[4 + (w + 8 - k) % 8]
            rcopy(v, v, g.ss.at[3 + k], g.rs.at[3 + k], g.at.sib).wait_recv()
        b = [g.B[4 + i] for i in range(8)]
        return ((b[0] + b[1]) + (b[2] + b[3])) + ((b[4] + b[5]) + (b[6] + b[7]))

    def drain(g):
        for k in range(1, 11):
            i = 0 if k < 4 else 1
            rcopy(g.S.at[i], g.B.at[0], g.ss.at[k], g.rs.at[k], g.at.sib).wait_send()


def norm_parts(v):
    c = v - jnp.mean(v, axis=-1, keepdims=True)
    r = lax.rsqrt(jnp.mean(c * c, axis=-1, keepdims=True) + 1e-05)
    return c * r, r


def norm_back(grad, gain, xhat, r):
    dx = grad * gain
    m1 = jnp.mean(dx, axis=-1, keepdims=True)
    m2 = jnp.mean(dx * xhat, axis=-1, keepdims=True)
    return r * (dx - m1 - xhat * m2)


GC0 = 0.7978845608028654
GC1 = GC0 * 0.044715


def gelu_both(u):
    u2 = u * u
    t = jnp.tanh(u * (GC0 + GC1 * u2))
    half = 0.5 + 0.5 * t
    slope = half + (0.5 * u) * (1.0 - t * t) * (GC0 + (3.0 * GC1) * u2)
    return u * half, slope


def halves(v):
    lane = lax.broadcasted_iota(jnp.int32, v.shape, 1)
    zero = jnp.zeros_like(v)
    return jnp.where(lane < HD, v, zero), jnp.where(lane >= HD, v, zero)


def vec(ref, name, start=0, n=None):
    at, whole = OFF[name]
    n = n or whole
    return ref[at + start : at + start + n].reshape(1, n)


GROUPS = ((3, 4, 5), (0, 1, 2))
NSLOT = 16
A, B, A0, A1, A2, B3, B4, B5, V, O, U0, U1, U2, U3, D0, D1, D2, D3 = range(18)
GATHER_IN = ((B3, 384, 768, 128), (B4, 512, 768, 128), (B5, 640, 768, 128), (A, 0, 768, 384), (V, 1536, 256, 256))
REDUCE_IN = ((B, 384, 768, 384), (A0, 0, 768, 128), (A1, 128, 768, 128), (A2, 256, 768, 128), (V, 1536, 256, 256))
GS, GZ, GX, GY, GD, GC, GF, GW, RS, RC, RD, RX, RZ, RF, ES, E = range(18, 34)
(
    AFTER_GIN,
    AFTER_GIN_V,
    AFTER_GOUT,
    AFTER_UP,
    ATTEND,
    BACK,
    BEFORE_DOWN,
    BEFORE_FFN,
    BEFORE_GIN,
    BEFORE_GIN_V,
    BEFORE_GOUT,
    BEFORE_MID,
    BEFORE_OUT,
    BEFORE_PROJECT,
    BEFORE_UP,
    LAST,
    MID_FFN,
    NORM,
    START,
    TAIL,
) = range(34, 54)


def block_kernel(comm, T, *refs):
    (length_ref, x_in, fv_in, ct_in, vec_ref, wi_in, wo_in, wu_in, wd_in) = refs[:9]
    (res, gt, gval, gi_out, go_out, gu_out, gd_out, ge_out, gl_out, keep) = refs[9:19]
    (Wi, Wo, Wu, Wd, Gi, Go, xa, du, h, q, k, v, oT, lse, h1, h2, dh, dy, dkT, dvT, ge, gl, pad, ls) = refs[19:43]
    length = length_ref[0]
    RB = 256
    FR, GR = 512, 768

    loads = [
        pltpu.make_async_copy(x_in, xa, ls.at[0]),
        pltpu.make_async_copy(fv_in, v.at[:, VH * HD :], ls.at[1]),
        pltpu.make_async_copy(ct_in, dy, ls.at[2]),
    ]
    for c in loads:
        c.start()

    if comm:
        (Ri, Ra, Rv, Ro, Ru, Rd, Xi, Xa, Xv, Xo, Xu, Xd, Fi, Fa, Fv, Fo, Fu, Fd, Pi, Po, Pu, Pd) = refs[43:65]
        (SE, BE, SL, BL, gss, grs, rss, rrs, ess, ers, els, vss, vrs) = refs[65:78]
        at = Place()
        core = at.c
        pre = []
        for i, (src, buf) in enumerate(((wi_in, Pi), (wo_in, Po), (wu_in, Pu), (wd_in, Pd))):
            local = pltpu.make_async_copy(src, buf.at[core], els.at[i])
            local.start()
            pre.append(local)
        entry_barrier(at)
        for i, (src, buf) in enumerate(((wi_in, Pi), (wo_in, Po), (wu_in, Pu), (wd_in, Pd))):
            pre[i].wait()
            pre[i] = rcopy(buf.at[core], buf.at[core], ess.at[i], ers.at[i], at.sib)
            pre[i].start()

        def pack(buf, W, rows, cols):
            both = jnp.concatenate([buf[0, :, cols], buf[1, :, cols]], axis=0)
            W[blk(at.chip, rows), cols] = both.astype(bf)

        def ready(i):
            pre[i].wait()

        gat, red = {}, {}
        for slot, (name, col0, stride, hc) in enumerate(GATHER_IN):
            gat[name] = Gather(at, Wi, col0, stride, hc, 48, gss.at[slot], grs.at[slot], False)
        where = {B: (Ri, Xi, Fi), V: (Rv, Xv, Fv)}
        for i in range(3):
            where[A0 + i] = (Ra.at[i], Xa.at[i], Fa.at[i])
        for slot, (name, col0, stride, hc) in enumerate(REDUCE_IN):
            red[name] = Reduce(at, Gi, col0, stride, hc, 48, *where[name], rss.at[slot], rrs.at[slot])
        slot = len(GATHER_IN)
        gat[O] = Gather(at, Wo, 0, 384, 384, 48, gss.at[slot], grs.at[slot], True)
        red[O] = Reduce(at, Go, 0, 384, 384, 48, Ro, Xo, Fo, rss.at[slot], rrs.at[slot])
        slot += 1
        for b in range(NB):
            gat[U0 + b] = Gather(at, Wu, FB * b, 384, 384, 48, gss.at[slot], grs.at[slot], True)
            red[U0 + b] = Reduce(at, Wu, FB * b, 384, 384, 48, Ru.at[b], Xu.at[b], Fu.at[b], rss.at[slot], rrs.at[slot])
            slot += 1
            gat[D0 + b] = GatherPlane(at, Wd, b, 384, 192, gss.at[slot], grs.at[slot])
            red[D0 + b] = ReducePlane(at, Wd, b, 384, 192, Rd.at[b], Xd.at[b], Fd, rss.at[slot], rrs.at[slot])
            slot += 1

        packed = set()

        def g_start(name):
            if name <= V:
                if 0 not in packed:
                    ready(0)
                    packed.add(0)
                if name == V:
                    pack_v()
                else:
                    pack(Pi, Wi, 48, gat[name].cols(core))
            elif name == O:
                ready(1)
                pack(Po, Wo, 48, gat[name].cols(core))
            elif name < D0:
                if 2 not in packed:
                    ready(2)
                    packed.add(2)
                pack(Pu, Wu, 48, gat[name].cols(core))
            elif 3 not in packed:
                ready(3)
                packed.add(3)
                pack(Pd, Wd, 192, lanes(core * 384, 384))
            gat[name].start()

        def pack_v():
            for hc in range(2):

                @pl.when(core == hc)
                def _():
                    c0 = 1536 + 256 * hc
                    n = min(256, WIN - c0)
                    both = jnp.concatenate([Pi[0, :, c0 : c0 + n], Pi[1, :, c0 : c0 + n]], axis=0).astype(bf)
                    if n < 256:
                        both = jnp.concatenate([both, jnp.zeros((48, 256 - n), bf)], axis=1)
                    Wi[blk(at.chip, 48), c0 : c0 + 256] = both

        sumE = SumAll(at, SE, BE, vss.at[0], vrs.at[0])
        sumL = SumAll(at, SL, BL, vss.at[1], vrs.at[1])
        finals = []

        def f_out(name):
            g = red[name]
            if name <= V:
                out, n, cols = gi_out, 24, g.cols(core)
            elif name == O:
                out, n, cols = go_out, 24, lanes(core * 384, 384)
            elif name < D0:
                out, n, cols = gu_out, 24, lanes(g.col0 + core * 384, 384)
            else:
                out, n, cols = gd_out, 96, lanes(core * 384, 384)
            e = 4 + len(finals) // 2
            r = rcopy(g.F.at[pl.ds(pl.multiple_of((1 - core) * n, 8), n)], out.at[:, cols], ess.at[e], ers.at[e], at.sib)
            l = pltpu.make_async_copy(g.F.at[pl.ds(pl.multiple_of(core * n, 8), n)], out.at[:, cols], els.at[e])
            r.start()
            l.start()
            finals.extend([r, l])

        def run(op, name=None, *arg):
            if op == GS:
                g_start(name)
            elif op == RF:
                f_out(name)
            elif op == ES:
                SE[0] = ge[...]
                sumE.start()
            elif op == E:
                sumE.middle()
            elif op < RS:
                g = gat[name]
                {GZ: g.step_z, GX: g.step_x, GY: g.step_y, GD: g.step_d, GC: g.share, GF: g.finish, GW: g.drain}[op](*arg)
            else:
                g = red[name]
                {RS: g.start, RC: g.step_c, RD: g.step_d, RX: g.step_xy, RZ: g.step_z}[op](*arg)

    else:
        ws = [pltpu.make_async_copy(a, b, ls.at[5 + i]) for i, (a, b) in enumerate(((wi_in, Wi), (wo_in, Wo), (wu_in, Wu), (wd_in, Wd)))]
        for c in ws:
            c.start()
        for c in ws:
            c.wait()

    def pump(*point):
        if comm:
            for step in SCHEDULE[point]:
                run(*step)

    pump(START)
    loads[0].wait()

    def norm_one(i, _):
        r = blk(i, RB)
        xh, _r = norm_parts(xa[r, :].astype(f32))
        h[r, :] = (xh * vec(vec_ref, "g1") + vec(vec_ref, "b1")).astype(bf)
        return 0

    lax.fori_loop(0, T // RB, norm_one, 0)
    loads[2].wait()

    def mask_rows(i, _):
        r = blk(i, RB)
        row = lax.broadcasted_iota(jnp.int32, (RB, 1), 0) + i * RB
        dy[r, :] = jnp.where(row < length, dy[r, :].astype(f32), 0.0).astype(bf)
        return 0

    lax.fori_loop(0, T // RB, mask_rows, 0)
    pump(NORM)

    eighth = jnp.asarray(0.125, bf)

    def project(group):
        fresh = group[0] < VH // 2
        c0 = PAIR * group[0]
        n = PAIR * len(group)
        qs, ks = slice(c0, c0 + n), slice(D + c0, D + c0 + n)

        def step(i, _):
            r = blk(i, RB * 2)
            hb = h[r, :]
            both = nn(hb, jnp.concatenate([Wi[:, qs], Wi[:, ks]], axis=1))
            q[r, qs] = (both[:, 0:n] + vec(vec_ref, "bq", c0, n)).astype(bf) * eighth
            k[r, qs] = both[:, n:].astype(bf)
            if fresh:
                vb = nn(hb, Wi[:, 2 * D : 2 * D + n]) + vec(vec_ref, "bv")
                v[r, qs] = vb.astype(bf)
            return 0

        lax.fori_loop(0, T // (RB * 2), step, 0)

    def pad_rows(i, _):
        r = blk(i, RB)
        row = lax.broadcasted_iota(jnp.int32, (RB, PAIR), 0) + i * RB
        lane = lax.broadcasted_iota(jnp.int32, (RB, PAIR), 1)
        pad[r, :] = jnp.where((lane == 0) & (row >= length), -1e9, 0.0).astype(bf)
        return 0

    lax.fori_loop(0, T // RB, pad_rows, 0)

    def scores(kp, qh, K):
        one = (lax.broadcasted_iota(jnp.int32, (QB, PAIR), 1) == 0).astype(f32).astype(bf)
        s = nt(kp, jnp.concatenate([qh, one], axis=1))
        key = lax.broadcasted_iota(jnp.int32, (QB, QB), 0)
        query = lax.broadcasted_iota(jnp.int32, (QB, QB), 1)
        last = jnp.where(key <= query, s[K - QB :], -1e9)
        return jnp.concatenate([s[0 : K - QB], last], axis=0) if K > QB else last

    def attend(p):
        c = blk(p, PAIR)
        vT = v[:, c].T
        for j in range(T // QB):
            if j != 1:
                pump(ATTEND, p, j)
            K = QB * (j + 1)
            rows = slice(QB * j, QB * j + QB)
            kp = jnp.concatenate([k[0:K, c], pad[0:K, :]], axis=1)
            for hd, qh in enumerate(halves(q[rows, c])):
                s = scores(kp, qh, K)
                top = jnp.max(s, axis=0, keepdims=True)
                e = jnp.exp(s - top)
                total = colsum(e)
                o = nn(vT[HD * hd : HD * hd + HD, 0:K], e.astype(bf))
                oT[pl.ds(pl.multiple_of(p * PAIR + HD * hd, HD), HD), rows] = (o / total).astype(bf)
                lse[2 * p + hd, :, rows] = top + jnp.log(total)

    loads[1].wait()
    for group in ((3,), (4,), (5,), (0, 1, 2)):
        pump(BEFORE_PROJECT, group[0])
        project(group)
        for p in group:
            attend(p)

    pump(BEFORE_OUT)

    def out_step(i, _):
        r = blk(i, RB)
        acc = xa[r, :].astype(f32) + vec(vec_ref, "bo") + tn(oT[:, r], Wo[...])
        h1[r, :] = acc
        xh, _r = norm_parts(acc)
        h2[r, :] = (xh * vec(vec_ref, "g2") + vec(vec_ref, "b2")).astype(bf)
        return 0

    lax.fori_loop(0, T // RB, out_step, 0)
    spill = pltpu.make_async_copy(h1, keep, ls.at[3])
    spill.start()
    unspill = pltpu.make_async_copy(keep, h1, ls.at[3])

    def put_early(name, value, at_=0):
        a = EARLY_AT[name] + at_
        ge[:, a : a + value.shape[1]] = value

    def put_late(name, value, at_=0):
        a = LATE_AT[name] + at_
        gl[:, a : a + value.shape[1]] = value

    for b in range(NB):
        pump(BEFORE_FFN, b)
        cu = slice(FB * b, FB * b + FB)
        if b == 0:
            spill.wait()

        def ffn(i, _, b=b, cu=cu):
            r = blk(i, FR)
            u = nn(h2[r, :], Wu[:, cu]) + vec(vec_ref, "bu", FB * b, FB)
            a, slope = gelu_both(u)
            ab = a.astype(bf)
            da = nt(dy[r, :], Wd[cu, :])
            dub = (slope * da).astype(bf)
            xa[r, :] = ab
            du[r, :] = dub
            feed = nn(ab, Wd[cu, :])
            if b < NB - 1:
                h1[r, :] += feed
            else:
                row = lax.broadcasted_iota(jnp.int32, (FR, 1), 0) + i * FR
                y = h1[r, :] + (feed + vec(vec_ref, "bd"))
                h1[r, :] = jnp.where(row < length, y, 0.0)
            back = nt(dub, Wu[:, cu])
            if b == 0:
                dh[r, :] = back
            else:
                dh[r, :] += back
            return 0

        lax.fori_loop(0, T // FR // 2, ffn, 0)
        pump(MID_FFN, b)
        lax.fori_loop(T // FR // 2, T // FR, ffn, 0)
        pump(BEFORE_DOWN, b)

        def down(i, _, b=b):
            r = blk(i, GR)
            Wd[pl.ds(pl.multiple_of(FB * b + i * GR, GR), GR), :] = tn(xa[:, r], dy[...]).astype(bf)
            return 0

        def up(i, _, cu=cu):
            r = blk(i, GR)
            Wu[r, cu] = tn(h2[:, r], du[...]).astype(bf)
            return 0

        lax.fori_loop(0, D // GR, down, 0)
        pump(BEFORE_UP, b)
        lax.fori_loop(0, D // GR, up, 0)
        pump(AFTER_UP, b)
        put_early("bu", colsum(du[...].astype(f32)), FB * b)

    def round_rows(i, _):
        r = blk(i, RB)
        xa[r, :] = h1[r, :].astype(bf)
        return 0

    lax.fori_loop(0, T // RB, round_rows, 0)
    unspill.start()
    res_out = pltpu.make_async_copy(xa, res, ls.at[4])
    res_out.start()
    pump(BEFORE_MID)
    unspill.wait()
    res_out.wait()

    def mid(i, carry):
        dg, db, dbo, dbd = carry
        r = blk(i, RB)
        xh, rs = norm_parts(h1[r, :])
        d = dh[r, :]
        dyf = dy[r, :].astype(f32)
        d1 = dyf + norm_back(d, vec(vec_ref, "g2"), xh, rs)
        dh[r, :] = d1
        da = d1.astype(bf)
        du[r, :] = da
        xa[r, :] = nt(da, Wo[...]).astype(bf)
        return dg + colsum(d * xh), db + colsum(d), dbo + colsum(da.astype(f32)), dbd + colsum(dyf)

    z = jnp.zeros((1, D), f32)
    sums = lax.fori_loop(0, T // RB, mid, (z, z, z, z))
    for name, value in zip(("g2", "b2", "bo", "bd"), sums):
        put_early(name, value)
    pump(BEFORE_GOUT)

    def gout(i, _):
        r = blk(i, RB)
        Go[r, :] = nn(oT[r, :], du[...]).astype(bf)
        return 0

    lax.fori_loop(0, D // RB, gout, 0)
    pump(AFTER_GOUT)

    def attend_back(p):
        c = blk(p, PAIR)
        kT = k[:, c].T
        for j in range(T // QB):
            if j != 1:
                pump(BACK, p, j)
            K = QB * (j + 1)
            L = K - QB
            rows = slice(QB * j, QB * j + QB)
            kp = jnp.concatenate([k[0:K, c], pad[0:K, :]], axis=1)
            qb, db = q[rows, c], xa[rows, c]
            qT, dT = qb.T, db.T
            dqs = []
            for hd, (qh, dhd) in enumerate(zip(halves(qb), halves(db))):
                hs = slice(HD * hd, HD * hd + HD)
                s = scores(kp, qh, K)
                pr = jnp.exp(s - lse[2 * p + hd, :, rows])
                dp = nt(v[0:K, c], dhd)
                inner = colsum(pr * dp)
                dsb = (pr * (dp - inner)).astype(bf)
                dqs.append(0.125 * nn(kT[hs, 0:K], dsb))
                dk = nt(qT[hs, :], dsb)
                dv = nt(dT[hs, :], pr.astype(bf))
                if j:
                    dkT[hs, 0:L] += dk[:, 0:L]
                    dvT[hs, 0:L] += dv[:, 0:L]
                dkT[hs, L:K] = dk[:, L:]
                dvT[hs, L:K] = dv[:, L:]
            h2[rows, c] = jnp.concatenate(dqs, axis=0).T.astype(bf)
        for j in range(T // QB):
            rows = slice(QB * j, QB * j + QB)
            dy[rows, c] = dkT[:, rows].T.astype(bf)
            du[rows, c] = dvT[:, rows].T.astype(bf)

    def gin(columns, parts):
        n = parts[0][1].stop - parts[0][1].start

        def step(i, _):
            r = blk(i, GR)
            g = tn(h[:, r], jnp.concatenate([src[:, s] for src, s in parts], axis=1)).astype(bf)
            for at_, c in enumerate(columns):
                Gi[r, c : c + n] = g[:, at_ * n : at_ * n + n]
            return 0

        lax.fori_loop(0, D // GR, step, 0)

    if comm:
        Gi[:, WIN:] = jnp.zeros((D, WPAD - WIN), bf)
    val_out = pltpu.make_async_copy(du.at[:, VH * HD :], gval, ls.at[1])
    for p in (3, 4, 5, 0, 1, 2):
        attend_back(p)
        if p == 5:
            val_out.start()
            pump(BEFORE_GIN, 3)
            s = slice(VH * HD, D)
            gin((VH * HD, D + VH * HD), ((h2, s), (dy, s)))
            pump(AFTER_GIN, 3)
        if p < VH // 2:
            s = slice(PAIR * p, PAIR * p + PAIR)
            pump(BEFORE_GIN, 10 + p)
            gin((PAIR * p, D + PAIR * p), ((h2, s), (dy, s)))
            pump(AFTER_GIN, 10 + p)
    pump(BEFORE_GIN_V)
    gin((2 * D,), ((du, slice(0, VH * HD)),))
    pump(AFTER_GIN_V)
    x_back = pltpu.make_async_copy(x_in, xa, ls.at[0])
    x_back.start()
    put_late("bq", colsum(h2[...].astype(f32)))
    put_late("bv", colsum(du[:, 0 : VH * HD].astype(f32)))
    x_back.wait()

    def last(i, carry):
        dg, db = carry
        r = blk(i, RB)
        d = nt(h2[r, :], Wi[:, 0:D]) + nt(dy[r, :], Wi[:, D : 2 * D]) + nt(du[r, 0 : VH * HD], Wi[:, 2 * D : WIN])
        xh, rs = norm_parts(xa[r, :].astype(f32))
        g = dh[r, :] + norm_back(d, vec(vec_ref, "g1"), xh, rs)
        xa[r, :] = g.astype(bf)
        return dg + colsum(d * xh), db + colsum(d)

    z2 = (z, z)
    for i in range(T // RB):
        pump(LAST, i)
        z2 = lax.fori_loop(i, i + 1, last, z2)
    put_late("g1", z2[0])
    put_late("b1", z2[1])
    tok_out = pltpu.make_async_copy(xa, gt, ls.at[0])
    tok_out.start()
    pump(TAIL)
    if comm:
        squares = jnp.zeros((1, 1), f32)
        for F in [Fi, Fv, Fo] + [Fa.at[i] for i in range(3)] + [Fu.at[b] for b in range(NB)] + [Fd]:
            f = F[...]
            squares = squares + jnp.sum(colsum(f * f), axis=1, keepdims=True)
        gl[:, LATE_N:] = jnp.broadcast_to(squares, (1, 128))
        SL[0] = gl[...]
        sumL.start()
        sumL.middle()
        gl[...] = sumL.last()
        ge[...] = sumE.last()
    else:
        gl[:, LATE_N:] = jnp.zeros((1, 128), f32)
    ends = [
        pltpu.make_async_copy(ge, ge_out, ls.at[2]),
        pltpu.make_async_copy(gl, gl_out, ls.at[3]),
    ]
    if not comm:
        for i, (a, o) in enumerate(((Gi, gi_out), (Go, go_out), (Wu, gu_out), (Wd, gd_out))):
            ends.append(pltpu.make_async_copy(a, o, ls.at[5 + i]))
    for e in ends:
        e.start()
    if comm:
        for f in finals:
            f.wait()
        for name in gat:
            if name <= O:
                gat[name].drain()
        for name in red:
            red[name].drain()
        sumE.drain()
        sumL.drain()
    for e in ends:
        e.wait()
    val_out.wait()
    tok_out.wait()


SCHEDULE = {
    (START,): ((GS, B3), (GS, B4), (GS, B5), (GS, A),),
    (NORM,): ((GX, B3, 0), (GY, B3, 0), (GX, B4, 0), (GY, B4, 0), (GX, B5, 0), (GY, B5, 0),),
    (BEFORE_PROJECT, 3,): ((GS, V), (GZ, B3, 1), (GZ, B3, 2), (GZ, B3, 3), (GZ, B4, 3), (GX, A, 0), (GY, A, 0), (GZ, B4, 2), (GZ, B4, 1), (GD, B3, 0), (GZ, B5, 3), (GD, B4, 0), (GS, D0), (GZ, B5, 2), (GD, B5, 0), (GZ, B5, 1), (GX, V, 0), (GY, V, 0), (GX, B3, 1), (GY, B3, 1), (GZ, A, 3), (GX, B3, 2), (GY, B3, 2), (GX, B3, 3), (GY, B3, 3), (GX, B4, 3), (GY, B4, 3), (GX, B4, 2), (GX, B4, 1), (GX, B5, 3), (GD, A, 0), (GZ, A, 2), (GY, B4, 2), (GX, B5, 2), (GY, B4, 1), (GX, B5, 1), (GY, B5, 3), (GZ, A, 1), (GY, B5, 2), (GY, B5, 1), (GZ, V, 3), (GX, A, 3), (GD, V, 0), (GD, B3, 2), (GD, B3, 1), (GD, B3, 3), (GF, B3),),
    (ATTEND, 3, 0,): ((GS, O), (GD, B4, 1), (GD, B4, 2), (GD, B4, 3), (GD, B5, 1), (GD, B5, 3), (GX, A, 2), (GY, A, 2), (GY, A, 3), (GZ, V, 1), (GZ, V, 2), (GX, A, 1),),
    (ATTEND, 3, 2,): ((GD, B5, 2), (GY, A, 1), (GX, V, 3), (GY, V, 3),),
    (ATTEND, 3, 3,): ((GX, O, 0), (GY, O, 0),),
    (BEFORE_PROJECT, 4,): ((GS, U0), (GD, A, 2), (GY, V, 1), (GY, V, 2), (GF, B4),),
    (ATTEND, 4, 0,): ((GD, A, 1), (GD, A, 3), (GX, V, 1),),
    (ATTEND, 4, 2,): ((GX, V, 2), (GD, V, 3), (GZ, D0), (GD, O, 0),),
    (ATTEND, 4, 3,): ((GS, D1), (GD, V, 1), (GD, V, 2), (GZ, O, 3), (GX, U0, 0), (GY, U0, 0),),
    (BEFORE_PROJECT, 5,): ((GF, B5),),
    (ATTEND, 5, 0,): ((GZ, O, 2),),
    (ATTEND, 5, 2,): ((GZ, O, 1), (GZ, U0, 3),),
    (ATTEND, 5, 3,): ((GX, D0), (GY, D0),),
    (BEFORE_PROJECT, 0,): ((GS, U1), (GX, O, 2), (GX, O, 3), (GY, O, 3), (GZ, U0, 1), (GZ, U0, 2), (GD, U0, 0), (GF, A), (GF, V),),
    (ATTEND, 0, 0,): ((GX, O, 1), (GY, O, 1), (GY, O, 2), (GX, U0, 3), (GY, U0, 3),),
    (ATTEND, 0, 2,): ((GS, D2), (GD, D0), (GC, D0), (GX, U1, 0),),
    (ATTEND, 0, 3,): ((GD, O, 3), (GZ, D1), (GY, U1, 0),),
    (ATTEND, 1, 0,): ((GX, U0, 1), (GY, U0, 1), (GX, U0, 2), (GY, U0, 2), (GS, U2), (GZ, U1, 3),),
    (ATTEND, 1, 2,): ((GD, O, 1), (GD, O, 2), (GC, O), (GD, U0, 3), (GD, U1, 0), (GZ, U1, 2),),
    (ATTEND, 1, 3,): ((GZ, U1, 1),),
    (ATTEND, 2, 0,): ((GS, D3),),
    (ATTEND, 2, 2,): ((GD, U0, 1), (GD, U0, 2), (GC, U0), (GX, D1), (GY, D1),),
    (ATTEND, 2, 3,): ((GZ, D2), (GX, U2, 0), (GY, U2, 0), (GX, U1, 3), (GY, U1, 3),),
    (BEFORE_OUT,): ((GX, U1, 2), (GY, U1, 2), (GZ, U2, 3), (GF, O),),
    (BEFORE_FFN, 0,): ((GS, U3), (GD, D1), (GC, D1), (GX, U1, 1), (GY, U1, 1), (GZ, U2, 1), (GZ, U2, 2), (GF, U0), (GF, D0),),
    (MID_FFN, 0,): ((GD, U1, 1), (GD, U1, 2), (GD, U1, 3), (GC, U1), (GX, D2), (GY, D2), (GX, U2, 3), (GY, U2, 3), (GD, U2, 0), (GZ, D3), (GX, U3, 0), (GY, U3, 0), (GX, U2, 1), (GY, U2, 1),),
    (BEFORE_DOWN, 0,): ((GD, D2), (GC, D2), (GX, U2, 2), (GY, U2, 2), (GZ, U3, 1), (GZ, U3, 2), (GZ, U3, 3), (GW, D0),),
    (BEFORE_UP, 0,): ((GD, U2, 3), (RS, D0), (GW, U0),),
    (AFTER_UP, 0,): ((GY, D3), (RS, U0),),
    (BEFORE_FFN, 1,): ((GF, U1), (GF, D1),),
    (MID_FFN, 1,): ((GD, U2, 1), (GD, U2, 2), (GC, U2), (GX, D3), (GX, U3, 1), (GY, U3, 1), (GX, U3, 2), (GY, U3, 2), (GX, U3, 3), (GY, U3, 3), (GD, U3, 0), (RC, U0), (RC, D0),),
    (BEFORE_DOWN, 1,): ((GD, D3), (GC, D3), (GD, U3, 1), (GD, U3, 2), (GD, U3, 3), (GC, U3), (RD, U0, 2), (GW, D1),),
    (BEFORE_UP, 1,): ((RD, U0, 0), (RD, U0, 1), (RD, U0, 3), (RS, D1), (GW, U1),),
    (AFTER_UP, 1,): ((RS, U1),),
    (BEFORE_FFN, 2,): ((GF, U2), (GF, D2),),
    (MID_FFN, 2,): ((RX, U0, 1), (RX, U0, 2), (RX, U0, 3), (RX, U0, 0), (RD, D0), (RC, D1),),
    (BEFORE_DOWN, 2,): ((RC, U1), (GW, D2),),
    (BEFORE_UP, 2,): ((RX, D0), (RS, D2), (RZ, U0), (RF, U0), (GW, U2),),
    (AFTER_UP, 2,): ((RD, D1), (RS, U2),),
    (BEFORE_FFN, 3,): ((GF, U3), (GF, D3),),
    (MID_FFN, 3,): ((RD, U1, 0), (RD, U1, 1), (RD, U1, 2), (RD, U1, 3), (RC, U2), (RC, D2),),
    (BEFORE_DOWN, 3,): ((RX, U1, 1), (RX, U1, 2), (RX, U1, 3), (RX, U1, 0), (RX, D1), (RD, U2, 0), (RD, U2, 2), (GW, D3),),
    (BEFORE_UP, 3,): ((RZ, D0), (RD, U2, 1), (RD, U2, 3), (RS, D3), (GW, U3),),
    (AFTER_UP, 3,): ((RS, U3),),
    (BEFORE_MID,): (),
    (BEFORE_GOUT,): ((RZ, U1), (RF, U1), (RX, U2, 1), (RX, U2, 2), (RX, U2, 3), (RX, U2, 0), (RD, D2), (RC, U3), (RC, D3), (ES,),),
    (AFTER_GOUT,): ((RS, O),),
    (BACK, 3, 0,): (),
    (BACK, 3, 2,): ((RZ, D1),),
    (BACK, 3, 3,): ((RX, D2), (RD, U3, 0), (RD, U3, 2), (RC, O), (RZ, U2), (RF, U2), (RD, U3, 1), (RD, U3, 3),),
    (BACK, 4, 0,): (),
    (BACK, 4, 2,): ((RD, D3), (E,),),
    (BACK, 4, 3,): ((RD, O, 0), (RD, O, 2),),
    (BACK, 5, 0,): ((RD, O, 1), (RD, O, 3),),
    (BACK, 5, 2,): ((RZ, D2), (RX, U3, 1), (RX, U3, 2), (RX, U3, 3), (RX, U3, 0),),
    (BACK, 5, 3,): (),
    (BEFORE_GIN, 3,): ((RX, D3),),
    (AFTER_GIN, 3,): ((RX, O, 1), (RX, O, 2), (RX, O, 3), (RX, O, 0), (RS, B),),
    (BACK, 0, 0,): (),
    (BACK, 0, 2,): ((RZ, U3), (RF, U3),),
    (BACK, 0, 3,): ((RC, B),),
    (BEFORE_GIN, 10,): (),
    (AFTER_GIN, 10,): ((RS, A0),),
    (BACK, 1, 0,): (),
    (BACK, 1, 2,): ((RD, B, 0), (RD, B, 1), (RD, B, 2), (RD, B, 3), (RC, A0),),
    (BACK, 1, 3,): ((RZ, D3), (RF, D0),),
    (BEFORE_GIN, 11,): ((RZ, O), (RF, O),),
    (AFTER_GIN, 11,): ((RX, B, 1), (RX, B, 2), (RX, B, 3), (RX, B, 0), (RD, A0, 0), (RD, A0, 1), (RD, A0, 2), (RD, A0, 3), (RS, A1),),
    (BACK, 2, 0,): (),
    (BACK, 2, 2,): (),
    (BACK, 2, 3,): ((RX, A0, 1), (RX, A0, 2), (RX, A0, 3), (RX, A0, 0), (RC, A1),),
    (BEFORE_GIN, 12,): ((RZ, B), (RF, B),),
    (AFTER_GIN, 12,): ((RD, A1, 0), (RD, A1, 1), (RD, A1, 2), (RD, A1, 3), (RS, A2),),
    (BEFORE_GIN_V,): (),
    (AFTER_GIN_V,): ((RZ, A0), (RF, A0), (RS, V),),
    (LAST, 0,): (),
    (LAST, 1,): ((RX, A1, 1), (RX, A1, 2), (RX, A1, 3), (RX, A1, 0), (RC, A2),),
    (LAST, 2,): ((RC, V),),
    (LAST, 3,): ((RD, A2, 0), (RD, A2, 1), (RD, A2, 2), (RD, A2, 3), (RZ, A1), (RF, A1),),
    (TAIL,): ((RD, V, 0), (RD, V, 2), (RD, V, 3), (RD, V, 1), (RX, A2, 1), (RX, A2, 2), (RX, A2, 3), (RX, A2, 0), (RX, V, 1), (RX, V, 2), (RX, V, 3), (RX, V, 0), (RZ, A2), (RF, A2), (RZ, V), (RF, V),),
}


def block(comm, length, x, fv, ct, vectors, wi, wo, wu, wd):
    T = x.shape[0]
    V, S = pltpu.VMEM, pltpu.SemaphoreType.DMA
    hbm = pl.BlockSpec(memory_space=pl.ANY)
    shape = jax.ShapeDtypeStruct
    outs = [shape((T, D), bf), shape((T, D), bf), shape((T, (H - VH) * HD), bf)]
    if comm:
        outs += [shape((24, WPAD), f32), shape((24, D), f32), shape((24, FF), f32), shape((96, D), f32)]
    else:
        outs += [shape((D, WPAD), bf), shape((D, D), bf), shape((D, FF), bf), shape((FF, D), bf)]
    outs += [shape((1, EARLY_N), f32), shape((1, LATE_ALL), f32), shape((T, D), f32)]
    row = lambda: V((T, D), bf)
    full = lambda: V((T, D), f32)
    scratch = [V((D, WPAD), bf), V((D, D), bf), V((D, FF), bf), V((FF, D), bf), V((D, WPAD), bf), V((D, D), bf)]
    scratch += [row(), row(), row(), row(), row(), row(), V((D, T), bf), V((H, 1, T), f32), full(), row(), full(), row()]
    scratch += [V((PAIR, T), f32), V((PAIR, T), f32), V((1, EARLY_N), f32), V((1, LATE_ALL), f32), V((T, PAIR), bf), S((9,))]
    params = dict(vmem_limit_bytes=63 << 20)
    if comm:
        scratch += [V((D, 384), bf), V((3, D, 128), bf), V((D, 256), bf), V((D, 384), bf), V((NB, D, 384), bf), V((NB, D, 384), bf)]
        scratch += [V((15, 48, 384), bf), V((3, 15, 48, 128), bf), V((15, 48, 256), bf), V((15, 48, 384), bf)]
        scratch += [V((NB, 15, 48, 384), bf), V((NB, 6, 192, 384), bf)]
        scratch += [V((48, 384), f32), V((3, 48, 128), f32), V((48, 256), f32), V((48, 384), f32), V((NB, 48, 384), f32), V((192, 384), f32)]
        scratch += [V((2, 24, WIN), f32), V((2, 24, D), f32), V((2, 24, FF), f32), V((2, 96, D), f32)]
        scratch += [V((2, 1, EARLY_N), f32), V((12, 1, EARLY_N), f32), V((2, 1, LATE_ALL), f32), V((12, 1, LATE_ALL), f32)]
        scratch += [S((14, NSLOT))] * 4 + [S((20,)), S((20,)), S((20,)), S((2, 11)), S((2, 11))]
        params.update(collective_id=1, has_side_effects=True)
    specs = [pl.BlockSpec(memory_space=pltpu.SMEM), hbm, hbm, hbm, pl.BlockSpec(memory_space=pltpu.VMEM), hbm, hbm, hbm, hbm]
    return pl.pallas_call(
        functools.partial(block_kernel, comm, T),
        out_shape=outs,
        in_specs=specs,
        out_specs=[hbm] * len(outs),
        scratch_shapes=scratch,
        compiler_params=pltpu.CompilerParams(**params),
    )(length, x, fv, ct, vectors, wi, wo, wu, wd)


def adam_step(master, grad, first, second, shadow, rate, decay):
    moment = BETA_ONE * first + (1.0 - BETA_ONE) * grad
    square = BETA_TWO * second + (1.0 - BETA_TWO) * grad * grad
    moment_hat = moment / (1.0 - BETA_ONE**STEP)
    square_hat = square / (1.0 - BETA_TWO**STEP)
    updated = master - rate * (moment_hat / (jnp.sqrt(square_hat) + EPS_ADAM) + decay * master)
    average = SHADOW_RATE * shadow + (1.0 - SHADOW_RATE) * updated
    return (updated, moment, square, average)


RATES = (RATE_MATRIX, RATE_OUTPUT, RATE_MATRIX, RATE_MATRIX)


def adam_kernel(*refs):
    ins, moved, norm, outs, moves, rest = refs[:26], refs[26:29], refs[29], refs[30:50], refs[50:53], refs[53:]
    bufs, news, isem, osem = rest[:26], rest[26:46], rest[46], rest[47]
    order = [4, 5] + [j for i in range(4) for j in (i, 6 + i, 10 + i, 14 + i, 18 + i)] + [22, 23, 24, 25]
    loads = {j: pltpu.make_async_copy(ins[j], bufs[j], isem.at[j]) for j in order}
    for j in order:
        loads[j].start()
    passing = [pltpu.make_async_copy(a, v, osem.at[23 + i]) for i, (a, v) in enumerate(zip(moved, rest[48:51]))]
    for c in passing:
        c.start()
    stores = []

    def send(i):
        c = pltpu.make_async_copy(news[i], outs[i], osem.at[i])
        c.start()
        stores.append(c)

    loads[4].wait()
    loads[5].wait()
    ge, gl = bufs[4], bufs[5]
    e, l = ge[...], gl[:, 0:LATE_N]
    total = gl[:, LATE_N : LATE_N + 1] + jnp.sum(e * e, axis=1, keepdims=True) + jnp.sum(l * l, axis=1, keepdims=True)
    size = jnp.sqrt(total)
    norm[...] = size
    factor = jnp.minimum(1.0, CLIP / size)
    for i in range(4):
        for j in (i, 6 + i, 10 + i, 14 + i, 18 + i):
            loads[j].wait()
        n, m = bufs[6 + i].shape
        for r in range(0, n, 24):
            rs = slice(r, r + 24)
            state = (bufs[10 + i][rs, :], bufs[14 + i][rs, :], bufs[18 + i][rs, :])
            new = adam_step(bufs[6 + i][rs, :], factor * bufs[i][rs, 0:m], *state, RATES[i], DECAY_MATRIX)
            for j, value in enumerate(new):
                news[4 * i + j][rs, :] = value
        for j in range(4):
            send(4 * i + j)
        if i < 3:
            passing[i].wait()
            c = pltpu.make_async_copy(rest[48 + i], moves[i], osem.at[20 + i])
            c.start()
            stores.append(c)
    for j in range(22, 26):
        loads[j].wait()
    for where, ref in ((EARLY_AT, ge), (LATE_AT, gl)):
        for name, a in where.items():
            o, n = OFF[name]
            w, m1, m2, avg = (bufs[j][o : o + n].reshape(1, n) for j in range(22, 26))
            new = adam_step(w, factor * ref[:, a : a + n], m1, m2, avg, RATE_VECTOR, 0.0)
            for j, value in enumerate(new):
                news[16 + j][o : o + n] = value.reshape(n)
    for j in range(16, 20):
        send(j)
    for c in stores:
        c.wait()


def adam(grads, ge, gl, masters, firsts, seconds, shadows, vecs, moved):
    shape = lambda a: jax.ShapeDtypeStruct(a.shape, f32)
    hbm = pl.BlockSpec(memory_space=pl.ANY)
    outs = [shape(m) for m in masters for _ in range(4)] + [shape(vecs[0])] * 4
    args = [*grads, ge, gl, *masters, *firsts, *seconds, *shadows, *vecs]
    return pl.pallas_call(
        adam_kernel,
        out_shape=[jax.ShapeDtypeStruct((1, 1), f32)] + outs + [jax.ShapeDtypeStruct(a.shape, a.dtype) for a in moved],
        in_specs=[hbm] * (len(args) + 3),
        out_specs=[pl.BlockSpec(memory_space=pltpu.VMEM)] + [hbm] * (len(outs) + 3),
        scratch_shapes=[pltpu.VMEM(a.shape, f32) for a in args]
        + [pltpu.VMEM(o.shape, f32) for o in outs]
        + [pltpu.SemaphoreType.DMA((26,)), pltpu.SemaphoreType.DMA((26,))]
        + [pltpu.VMEM(a.shape, a.dtype) for a in moved],
        compiler_params=pltpu.CompilerParams(vmem_limit_bytes=60 << 20),
    )(*args, *moved)


def body(own_links, *args):
    tokens, first_values, cotangent, lengths = args[:4]
    masters, firsts, seconds, shadows = args[4:8], args[8:12], args[12:16], args[16:20]
    vectors, first_vectors, second_vectors, shadow_vectors = vecs = args[20:24]
    both = ("wide", "narrow")
    slots = tokens.shape[0]
    if own_links and slots == 1:
        got = block(True, lengths, tokens[0], first_values[0], cotangent[0], vectors, *masters)
        new = adam(got[3:7], got[7], got[8], masters, firsts, seconds, shadows, vecs, got[:3])
        return (*(a[None] for a in new[21:24]), new[0].reshape(()), *new[1:21])
    weights = [lax.all_gather(m.astype(bf), both, axis=0, tiled=True) for m in masters]
    weights[0] = jnp.pad(weights[0], ((0, 0), (0, WPAD - WIN)))
    per_slot = [
        block(False, lengths[i : i + 1], tokens[i], first_values[i], cotangent[i], vectors, *weights) for i in range(slots)
    ]
    result, grad_tokens, grad_values = (jnp.stack([s[i] for s in per_slot]) for i in range(3))
    totals = [sum(s[i].astype(f32) for s in per_slot) for i in range(3, 9)]
    totals[0] = totals[0][:, :WIN]
    shards = [lax.psum_scatter(g, both, scatter_dimension=0, tiled=True) for g in totals[:4]]
    squares = sum(jnp.sum(g * g) for g in shards)
    pieces = {n: totals[4][0, a : a + OFF[n][1]] for n, a in EARLY_AT.items()}
    pieces.update({n: totals[5][0, a : a + OFF[n][1]] for n, a in LATE_AT.items()})
    vector_grad, squares = lax.psum((jnp.concatenate([pieces[n] for n in OFF]), squares), both)
    grad_norm = jnp.sqrt(squares + jnp.sum(vector_grad * vector_grad))
    factor = jnp.minimum(1.0, CLIP / grad_norm)
    outputs = [result, grad_tokens, grad_values, grad_norm]
    for i in range(4):
        outputs.extend(adam_step(masters[i], factor * shards[i], firsts[i], seconds[i], shadows[i], RATES[i], DECAY_MATRIX))
    outputs.extend(adam_step(vectors, factor * vector_grad, first_vectors, second_vectors, shadow_vectors, RATE_VECTOR, 0.0))
    return tuple(outputs)


def solution(mesh):
    both = ("wide", "narrow")
    rows3, rows2 = P(both, None, None), P(both, None)
    own_links = (mesh.shape["wide"], mesh.shape["narrow"]) == (8, 4)
    return jax.shard_map(
        functools.partial(body, own_links),
        mesh=mesh,
        in_specs=(rows3,) * 3 + (P(both),) + (rows2,) * 16 + (P(),) * 4,
        out_specs=(rows3,) * 3 + (P(),) + (rows2,) * 16 + (P(),) * 4,
        check_vma=False,
    )
```

```python
import functools

import jax
import jax.numpy as jnp
from jax import lax
from jax.experimental import pallas as pl
from jax.experimental.pallas import tpu as pltpu
from jax.sharding import PartitionSpec as P

D = 768
H = 12
HD = 64
FF = 3072
VH = 6
STEP = 7
BETA_ONE = 0.5
BETA_TWO = 0.5
SHADOW_RATE = 0.5
RATE_MATRIX = 0.03
RATE_OUTPUT = 0.15
RATE_VECTOR = 0.3
DECAY_MATRIX = 0.1
CLIP = 1.0
EPS_ADAM = 1e-08

bf = jnp.bfloat16
f32 = jnp.float32
MESH = pl.DeviceIdType.MESH
WIN = 2 * D + VH * HD
WPAD = 2048
FB = 768
NB = FF // FB
QB = 256
PAIR = 2 * HD
PAIRS = H // 2

OFF = {}
_at = 0
for _name, _n in (("g1", D), ("b1", D), ("g2", D), ("b2", D), ("bq", D), ("bv", VH * HD), ("bo", D), ("bu", FF), ("bd", D)):
    OFF[_name] = (_at, _n)
    _at += _n
VEC = _at
EARLY = ("g2", "b2", "bo", "bu", "bd")
LATE = ("g1", "b1", "bq", "bv")


def offsets_in(names):
    where, at = {}, 0
    for name in names:
        where[name] = at
        at += OFF[name][1]
    return where, at


EARLY_AT, EARLY_N = offsets_in(EARLY)
LATE_AT, LATE_N = offsets_in(LATE)
LATE_ALL = LATE_N + 128


def nn(a, b):
    return lax.dot_general(a, b, (((1,), (0,)), ((), ())), preferred_element_type=f32)


def nt(a, b):
    return lax.dot_general(a, b, (((1,), (1,)), ((), ())), preferred_element_type=f32)


def tn(a, b):
    return lax.dot_general(a, b, (((0,), (0,)), ((), ())), preferred_element_type=f32)


def blk(i, n):
    return pl.ds(i * n if isinstance(i, int) else pl.multiple_of(i * n, n), n)


def lanes(start, n):
    return pl.ds(start if isinstance(start, int) else pl.multiple_of(start, 128), n)


def colsum(v):
    return jnp.sum(v, axis=0, keepdims=True)


class Place:
    def __init__(s):
        s.w = lax.axis_index("wide")
        s.n = lax.axis_index("narrow")
        s.z, s.y, s.x, s.c = s.w // 2, s.w % 2, s.n // 2, s.n % 2
        s.sib = (s.w, s.n + 1 - 2 * s.c)
        s.xn = (s.w, (s.n + 2) % 4)
        s.yn = (s.w + 1 - 2 * s.y, s.n)
        s.chip = s.z * 4 + s.y * 2 + s.x

    def zdev(s, zt):
        return (zt * 2 + s.y, s.n)

    def p(s, zt, dy, dx):
        yy = 1 - s.y if dy else s.y
        xx = 1 - s.x if dx else s.x
        return zt * 4 + yy * 2 + xx


def rcopy(src, dst, ss, rs, dev):
    return pltpu.make_async_remote_copy(
        src_ref=src, dst_ref=dst, send_sem=ss, recv_sem=rs, device_id=dev, device_id_type=MESH
    )


def entry_barrier(at):
    bar = pltpu.get_barrier_semaphore()
    for k in (1, 2, 3):
        pl.semaphore_signal(bar, inc=1, device_id=(at.w, (at.n + k) % 4), device_id_type=MESH)
    for k in range(1, 8):
        pl.semaphore_signal(bar, inc=1, device_id=((at.w + k) % 8, at.n), device_id_type=MESH)
    pl.semaphore_wait(bar, 10)


class Gather:
    def __init__(g, at, W, col0, stride, hc, rb, ss, rs, bulk):
        g.bulk = bulk
        g.at, g.W, g.col0, g.stride, g.hc, g.rb, g.ss, g.rs = at, W, col0, stride, hc, rb, ss, rs

    def cols(g, h):
        return lanes(g.col0 + h * g.stride, g.hc)

    def view(g, p):
        return g.W.at[blk(p, g.rb), g.cols(g.at.c)]

    def half(g, h):
        return g.W.at[:, g.cols(h)]

    def put(g, p, i, dev):
        if i == 15 and g.bulk:
            return
        v = g.view(p)
        rcopy(v, v, g.ss.at[i], g.rs.at[i], dev).start()

    def share(g):
        v = g.half(g.at.c)
        rcopy(v, v, g.ss.at[15], g.rs.at[15], g.at.sib).start()

    def got(g, p, i):
        v = g.view(p)
        rcopy(v, v, g.ss.at[i], g.rs.at[i], g.at.sib).wait_recv()

    def zk(g, k):
        return (g.at.z + 4 - k) % 4

    def spread(g, p, k):
        g.put(p, 3 + k, g.at.xn)
        g.put(p, 9 + k, g.at.yn)
        g.put(p, 15, g.at.sib)

    def start(g):
        p = g.at.chip
        for k in (1, 2, 3):
            g.put(p, k - 1, g.at.zdev((g.at.z + k) % 4))
        g.spread(p, 0)

    def step_z(g, k):
        p = g.at.p(g.zk(k), 0, 0)
        g.got(p, k - 1)
        g.spread(p, k)

    def step_x(g, k):
        p = g.at.p(g.zk(k), 0, 1)
        g.got(p, 3 + k)
        if k < 2:
            g.put(p, 13 + k, g.at.yn)
        g.put(p, 15, g.at.sib)

    def step_y(g, k):
        p = g.at.p(g.zk(k), 1, 0)
        g.got(p, 9 + k)
        if k >= 2:
            g.put(p, 5 + k, g.at.xn)
        g.put(p, 15, g.at.sib)

    def step_d(g, k):
        p = g.at.p(g.zk(k), 1, 1)
        g.got(p, 13 + k if k < 2 else 5 + k)
        g.put(p, 15, g.at.sib)

    def finish(g):
        v = g.half(1 - g.at.c)
        rcopy(v, v, g.ss.at[15], g.rs.at[15], g.at.sib).wait_recv()

    def drain(g):
        v = g.view(g.at.chip)
        for i in range(15):
            rcopy(v, v, g.ss.at[i], g.rs.at[i], g.at.sib).wait_send()
        v = g.half(g.at.c)
        rcopy(v, v, g.ss.at[15], g.rs.at[15], g.at.sib).wait_send()


class GatherPlane:
    def __init__(g, at, W, b, hc, rb, ss, rs):
        g.bulk = True
        g.at, g.W, g.b, g.hc, g.rb, g.ss, g.rs = at, W, b, hc, rb, ss, rs

    def view(g, p, part=None):
        n = g.rb if part is None else g.rb // 2
        r0 = p * g.rb if part is None else p * g.rb + part * n
        return g.W.at[pl.ds(pl.multiple_of(r0, n), n), lanes(g.at.c * g.hc, g.hc)]

    def half(g, h):
        return g.W.at[pl.ds(g.b * 4 * g.rb, 4 * g.rb), lanes(h * g.hc, g.hc)]

    def share(g):
        v = g.half(g.at.c)
        rcopy(v, v, g.ss.at[15], g.rs.at[15], g.at.sib).start()

    def put(g, p, i, dev, part=None):
        if i == 15:
            return
        v = g.view(p, part)
        rcopy(v, v, g.ss.at[i], g.rs.at[i], dev).start()

    def got(g, p, i, part=None):
        v = g.view(p, part)
        rcopy(v, v, g.ss.at[i], g.rs.at[i], g.at.sib).wait_recv()

    def start(g):
        at = g.at

        @pl.when(at.z == g.b)
        def _():
            for k in (1, 2, 3):
                g.put(at.chip, k - 1, at.zdev((at.z + k) % 4))

    def step_z(g):
        at = g.at
        p = at.p(g.b, 0, 0)

        @pl.when(at.z != g.b)
        def _():
            k = (at.z + 4 - g.b) % 4
            v = g.view(p)
            rcopy(v, v, g.ss.at[k - 1], g.rs.at[k - 1], at.sib).wait_recv()

        g.put(p, 3, at.xn)
        g.put(p, 4, at.yn)
        g.put(p, 15, at.sib)

    def step_x(g):
        p = g.at.p(g.b, 0, 1)
        g.got(p, 3)
        g.put(p, 5, g.at.yn, 0)
        g.put(p, 15, g.at.sib)

    def step_y(g):
        p = g.at.p(g.b, 1, 0)
        g.got(p, 4)
        g.put(p, 6, g.at.xn, 1)
        g.put(p, 15, g.at.sib)

    def step_d(g):
        pd = g.at.p(g.b, 1, 1)
        g.got(pd, 5, 0)
        g.got(pd, 6, 1)
        g.put(pd, 15, g.at.sib)

    def finish(g):
        v = g.half(1 - g.at.c)
        rcopy(v, v, g.ss.at[15], g.rs.at[15], g.at.sib).wait_recv()

    def drain(g):
        at = g.at
        v = g.view(at.chip)

        @pl.when(at.z == g.b)
        def _():
            for i in range(3):
                rcopy(v, v, g.ss.at[i], g.rs.at[i], at.sib).wait_send()

        for i in (3, 4):
            rcopy(v, v, g.ss.at[i], g.rs.at[i], at.sib).wait_send()
        v = g.view(at.chip, 0)
        for i in (5, 6):
            rcopy(v, v, g.ss.at[i], g.rs.at[i], at.sib).wait_send()
        v = g.half(at.c)
        rcopy(v, v, g.ss.at[15], g.rs.at[15], at.sib).wait_send()


class Reduce:
    def __init__(g, at, G, col0, stride, hc, rb, R, X, F, ss, rs):
        g.at, g.G, g.col0, g.stride, g.hc, g.rb = at, G, col0, stride, hc, rb
        g.R, g.X, g.F, g.ss, g.rs = R, X, F, ss, rs

    def cols(g, h):
        return lanes(g.col0 + h * g.stride, g.hc)

    def mine(g):
        return g.cols(g.at.c)

    def view(g, p):
        return g.G.at[blk(p, g.rb), g.mine()]

    def load(g, p):
        return g.G[blk(p, g.rb), g.mine()].astype(f32)

    def store(g, p, v):
        g.G[blk(p, g.rb), g.mine()] = v.astype(bf)

    def first(g):
        return rcopy(g.G.at[:, g.cols(1 - g.at.c)], g.R, g.ss.at[15], g.rs.at[15], g.at.sib)

    def start(g):
        g.first().start()

    def put(g, p, i, dev):
        rcopy(g.view(p), g.X.at[i], g.ss.at[i], g.rs.at[i], dev).start()

    def got(g, i):
        v = g.X.at[i]
        rcopy(v, v, g.ss.at[i], g.rs.at[i], g.at.sib).wait_recv()

    def add_core(g, p):
        g.store(p, g.load(p) + g.R[blk(p, g.rb), :].astype(f32))

    def step_c(g):
        at = g.at
        g.first().wait_recv()
        for zt in range(4):
            p = at.p(zt, 1, 1)
            g.add_core(p)
            g.put(p, zt, at.yn if zt < 2 else at.xn)
        for zt in range(4):
            p = at.p(zt, 1, 0) if zt < 2 else at.p(zt, 0, 1)
            g.add_core(p)
            if zt < 2:
                g.put(p, 8 + zt, at.yn)
            else:
                g.put(p, 4 + zt, at.xn)

    def step_d(g, zt):
        at = g.at
        p = at.p(zt, 0, 1) if zt < 2 else at.p(zt, 1, 0)
        g.got(zt)
        g.store(p, g.load(p) + (g.R[blk(p, g.rb), :].astype(f32) + g.X[zt].astype(f32)))
        if zt < 2:
            g.put(p, 4 + zt, at.xn)
        else:
            g.put(p, 8 + zt, at.yn)

    def step_xy(g, k):
        at = g.at
        zt = (at.z + k) % 4
        g.got(4 + zt)
        g.got(8 + zt)
        p = at.p(zt, 0, 0)
        s = g.load(p) + g.R[blk(p, g.rb), :].astype(f32)
        s = s + (g.X[4 + zt].astype(f32) + g.X[8 + zt].astype(f32))
        if k:
            g.store(p, s)
            g.put(p, 11 + k, at.zdev(zt))
        else:
            g.F[...] = s

    def step_z(g):
        s = g.F[...]
        for k in (1, 2, 3):
            g.got(11 + k)
            s = s + g.X[11 + k].astype(f32)
        g.F[...] = s

    def drain(g):
        for i in range(15):
            rcopy(g.view(g.at.chip), g.X.at[i], g.ss.at[i], g.rs.at[i], g.at.sib).wait_send()
        g.first().wait_send()


class ReducePlane:
    def __init__(g, at, G, b, hc, rb, R, X, F, ss, rs):
        g.at, g.G, g.b, g.hc, g.rb, g.R, g.X, g.F, g.ss, g.rs = at, G, b, hc, rb, R, X, F, ss, rs

    def cols(g, h):
        return lanes(h * g.hc, g.hc)

    def span(g, p, part=None, local=False):
        n = g.rb
        r0 = (p - 4 * g.b) * n if local else p * n
        if part is not None:
            n = n // 2
            r0 = r0 + part * n
        return pl.ds(pl.multiple_of(r0, n), n)

    def first(g):
        src = g.G.at[pl.ds(g.b * 4 * g.rb, 4 * g.rb), g.cols(1 - g.at.c)]
        return rcopy(src, g.R, g.ss.at[15], g.rs.at[15], g.at.sib)

    def start(g):
        g.first().start()

    def copy(g, p, i, slot, dev, part=None):
        src = g.G.at[g.span(p, part), g.cols(g.at.c)]
        dst = g.X.at[i]
        if part is not None:
            dst = g.X.at[i, pl.ds(part * (g.rb // 2), g.rb // 2)]
        return rcopy(src, dst, g.ss.at[slot], g.rs.at[slot], dev)

    def load(g, p, part=None):
        return g.G[g.span(p, part), g.cols(g.at.c)].astype(f32)

    def store(g, p, v, part=None):
        g.G[g.span(p, part), g.cols(g.at.c)] = v.astype(bf)

    def add_core(g, p):
        g.store(p, g.load(p) + g.R[g.span(p, None, True), :].astype(f32))

    def step_c(g):
        at = g.at
        g.first().wait_recv()
        pd = at.p(g.b, 1, 1)
        g.add_core(pd)
        g.copy(pd, 0, 0, at.yn, 0).start()
        g.copy(pd, 0, 1, at.xn, 1).start()
        g.add_core(at.p(g.b, 0, 1))
        g.add_core(at.p(g.b, 1, 0))

    def step_d(g):
        at = g.at
        h = g.rb // 2
        for part, p, slot, dev, i in ((0, at.p(g.b, 0, 1), 0, at.xn, 1), (1, at.p(g.b, 1, 0), 1, at.yn, 2)):
            g.copy(p, 0, slot, at.sib, part).wait_recv()
            g.store(p, g.load(p, part) + g.X[0, part * h : part * h + h].astype(f32), part)
            g.copy(p, i, 1 + i, dev).start()

    def step_xy(g):
        at = g.at
        p = at.p(g.b, 0, 0)
        g.copy(p, 1, 2, at.sib).wait_recv()
        g.copy(p, 2, 3, at.sib).wait_recv()
        s = g.load(p) + g.R[g.span(p, None, True), :].astype(f32)
        s = s + (g.X[1].astype(f32) + g.X[2].astype(f32))

        @pl.when(at.z == g.b)
        def _():
            g.F[...] = s

        @pl.when(at.z != g.b)
        def _():
            g.store(p, s)
            k = (at.z + 4 - g.b) % 4
            src = g.G.at[g.span(p), g.cols(at.c)]
            rcopy(src, g.X.at[2 + k], g.ss.at[4], g.rs.at[3 + k], at.zdev(g.b)).start()

    def step_z(g):
        at = g.at

        @pl.when(at.z == g.b)
        def _():
            s = g.F[...]
            for k in (1, 2, 3):
                v = g.X.at[2 + k]
                rcopy(v, v, g.ss.at[4], g.rs.at[3 + k], at.sib).wait_recv()
                s = s + g.X[2 + k].astype(f32)
            g.F[...] = s

    def drain(g):
        at = g.at
        p = at.chip
        g.copy(p, 0, 0, at.sib, 0).wait_send()
        g.copy(p, 0, 1, at.sib, 1).wait_send()
        g.copy(p, 1, 2, at.sib).wait_send()
        g.copy(p, 2, 3, at.sib).wait_send()

        @pl.when(at.z != g.b)
        def _():
            g.copy(p, 1, 4, at.sib).wait_send()

        g.first().wait_send()


class SumAll:
    def __init__(g, at, S, B, ss, rs):
        g.at, g.S, g.B, g.ss, g.rs = at, S, B, ss, rs

    def start(g):
        n = g.at.n
        for k in (1, 2, 3):
            rcopy(g.S.at[0], g.B.at[n], g.ss.at[k], g.rs.at[k], (g.at.w, (n + k) % 4)).start()
        g.B[n] = g.S[0]

    def middle(g):
        w, n = g.at.w, g.at.n
        for k in (1, 2, 3):
            v = g.B.at[(n + 4 - k) % 4]
            rcopy(v, v, g.ss.at[k], g.rs.at[k], g.at.sib).wait_recv()
        total = (g.B[0] + g.B[1]) + (g.B[2] + g.B[3])
        g.S[1] = total
        for k in range(1, 8):
            rcopy(g.S.at[1], g.B.at[4 + w], g.ss.at[3 + k], g.rs.at[3 + k], ((w + k) % 8, n)).start()
        g.B[4 + w] = total

    def last(g):
        w = g.at.w
        for k in range(1, 8):
            v = g.B.at[4 + (w + 8 - k) % 8]
            rcopy(v, v, g.ss.at[3 + k], g.rs.at[3 + k], g.at.sib).wait_recv()
        b = [g.B[4 + i] for i in range(8)]
        return ((b[0] + b[1]) + (b[2] + b[3])) + ((b[4] + b[5]) + (b[6] + b[7]))

    def drain(g):
        for k in range(1, 11):
            i = 0 if k < 4 else 1
            rcopy(g.S.at[i], g.B.at[0], g.ss.at[k], g.rs.at[k], g.at.sib).wait_send()


def norm_parts(v):
    c = v - jnp.mean(v, axis=-1, keepdims=True)
    r = lax.rsqrt(jnp.mean(c * c, axis=-1, keepdims=True) + 1e-05)
    return c * r, r


def norm_back(grad, gain, xhat, r):
    dx = grad * gain
    m1 = jnp.mean(dx, axis=-1, keepdims=True)
    m2 = jnp.mean(dx * xhat, axis=-1, keepdims=True)
    return r * (dx - m1 - xhat * m2)


GC0 = 0.7978845608028654
GC1 = GC0 * 0.044715


def gelu_both(u):
    u2 = u * u
    t = jnp.tanh(u * (GC0 + GC1 * u2))
    half = 0.5 + 0.5 * t
    slope = half + (0.5 * u) * (1.0 - t * t) * (GC0 + (3.0 * GC1) * u2)
    return u * half, slope


def halves(v):
    lane = lax.broadcasted_iota(jnp.int32, v.shape, 1)
    zero = jnp.zeros_like(v)
    return jnp.where(lane < HD, v, zero), jnp.where(lane >= HD, v, zero)


def vec(ref, name, start=0, n=None):
    at, whole = OFF[name]
    n = n or whole
    return ref[at + start : at + start + n].reshape(1, n)


GROUPS = ((3, 4, 5), (0, 1, 2))
NSLOT = 16
A, B, A0, A1, A2, B3, B4, B5, V, O, U0, U1, U2, U3, D0, D1, D2, D3 = range(18)
GATHER_IN = ((B3, 384, 768, 128), (B4, 512, 768, 128), (B5, 640, 768, 128), (A, 0, 768, 384), (V, 1536, 256, 256))
REDUCE_IN = ((B, 384, 768, 384), (A0, 0, 768, 128), (A1, 128, 768, 128), (A2, 256, 768, 128), (V, 1536, 256, 256))
GS, GZ, GX, GY, GD, GC, GF, GW, RS, RC, RD, RX, RZ, RF, ES, E = range(18, 34)
(
    AFTER_GIN,
    AFTER_GIN_V,
    AFTER_GOUT,
    AFTER_UP,
    ATTEND,
    BACK,
    BEFORE_DOWN,
    BEFORE_FFN,
    BEFORE_GIN,
    BEFORE_GIN_V,
    BEFORE_GOUT,
    BEFORE_MID,
    BEFORE_OUT,
    BEFORE_PROJECT,
    BEFORE_UP,
    LAST,
    MID_FFN,
    NORM,
    START,
    TAIL,
) = range(34, 54)


def block_kernel(comm, T, *refs):
    (length_ref, x_in, fv_in, ct_in, vec_ref, wi_in, wo_in, wu_in, wd_in) = refs[:9]
    (res, gt, gval, gi_out, go_out, gu_out, gd_out, ge_out, gl_out, keep) = refs[9:19]
    (Wi, Wo, Wu, Wd, Gi, Go, xa, du, h, q, k, v, oT, lse, h1, h2, dh, dy, dkT, dvT, ge, gl, pad, ls) = refs[19:43]
    length = length_ref[0]
    RB = 256
    FR, GR = 512, 768

    loads = [
        pltpu.make_async_copy(x_in, xa, ls.at[0]),
        pltpu.make_async_copy(fv_in, v.at[:, VH * HD :], ls.at[1]),
        pltpu.make_async_copy(ct_in, dy, ls.at[2]),
    ]
    for c in loads:
        c.start()

    if comm:
        (Ri, Ra, Rv, Ro, Ru, Rd, Xi, Xa, Xv, Xo, Xu, Xd, Fi, Fa, Fv, Fo, Fu, Fd, Pi, Po, Pu, Pd) = refs[43:65]
        (SE, BE, SL, BL, gss, grs, rss, rrs, ess, ers, els, vss, vrs) = refs[65:78]
        at = Place()
        core = at.c
        pre = []
        for i, (src, buf) in enumerate(((wi_in, Pi), (wo_in, Po), (wu_in, Pu), (wd_in, Pd))):
            local = pltpu.make_async_copy(src, buf.at[core], els.at[i])
            local.start()
            pre.append(local)
        entry_barrier(at)
        for i, (src, buf) in enumerate(((wi_in, Pi), (wo_in, Po), (wu_in, Pu), (wd_in, Pd))):
            pre[i].wait()
            pre[i] = rcopy(buf.at[core], buf.at[core], ess.at[i], ers.at[i], at.sib)
            pre[i].start()

        def pack(buf, W, rows, cols):
            both = jnp.concatenate([buf[0, :, cols], buf[1, :, cols]], axis=0)
            W[blk(at.chip, rows), cols] = both.astype(bf)

        def ready(i):
            pre[i].wait()

        gat, red = {}, {}
        for slot, (name, col0, stride, hc) in enumerate(GATHER_IN):
            gat[name] = Gather(at, Wi, col0, stride, hc, 48, gss.at[slot], grs.at[slot], False)
        where = {B: (Ri, Xi, Fi), V: (Rv, Xv, Fv)}
        for i in range(3):
            where[A0 + i] = (Ra.at[i], Xa.at[i], Fa.at[i])
        for slot, (name, col0, stride, hc) in enumerate(REDUCE_IN):
            red[name] = Reduce(at, Gi, col0, stride, hc, 48, *where[name], rss.at[slot], rrs.at[slot])
        slot = len(GATHER_IN)
        gat[O] = Gather(at, Wo, 0, 384, 384, 48, gss.at[slot], grs.at[slot], True)
        red[O] = Reduce(at, Go, 0, 384, 384, 48, Ro, Xo, Fo, rss.at[slot], rrs.at[slot])
        slot += 1
        for b in range(NB):
            gat[U0 + b] = Gather(at, Wu, FB * b, 384, 384, 48, gss.at[slot], grs.at[slot], True)
            red[U0 + b] = Reduce(at, Wu, FB * b, 384, 384, 48, Ru.at[b], Xu.at[b], Fu.at[b], rss.at[slot], rrs.at[slot])
            slot += 1
            gat[D0 + b] = GatherPlane(at, Wd, b, 384, 192, gss.at[slot], grs.at[slot])
            red[D0 + b] = ReducePlane(at, Wd, b, 384, 192, Rd.at[b], Xd.at[b], Fd, rss.at[slot], rrs.at[slot])
            slot += 1

        packed = set()

        def g_start(name):
            if name <= V:
                if 0 not in packed:
                    ready(0)
                    packed.add(0)
                if name == V:
                    pack_v()
                else:
                    pack(Pi, Wi, 48, gat[name].cols(core))
            elif name == O:
                ready(1)
                pack(Po, Wo, 48, gat[name].cols(core))
            elif name < D0:
                if 2 not in packed:
                    ready(2)
                    packed.add(2)
                pack(Pu, Wu, 48, gat[name].cols(core))
            elif 3 not in packed:
                ready(3)
                packed.add(3)
                pack(Pd, Wd, 192, lanes(core * 384, 384))
            gat[name].start()

        def pack_v():
            for hc in range(2):

                @pl.when(core == hc)
                def _():
                    c0 = 1536 + 256 * hc
                    n = min(256, WIN - c0)
                    both = jnp.concatenate([Pi[0, :, c0 : c0 + n], Pi[1, :, c0 : c0 + n]], axis=0).astype(bf)
                    if n < 256:
                        both = jnp.concatenate([both, jnp.zeros((48, 256 - n), bf)], axis=1)
                    Wi[blk(at.chip, 48), c0 : c0 + 256] = both

        sumE = SumAll(at, SE, BE, vss.at[0], vrs.at[0])
        sumL = SumAll(at, SL, BL, vss.at[1], vrs.at[1])
        finals = []

        def f_out(name):
            g = red[name]
            if name <= V:
                out, n, cols = gi_out, 24, g.cols(core)
            elif name == O:
                out, n, cols = go_out, 24, lanes(core * 384, 384)
            elif name < D0:
                out, n, cols = gu_out, 24, lanes(g.col0 + core * 384, 384)
            else:
                out, n, cols = gd_out, 96, lanes(core * 384, 384)
            e = 4 + len(finals) // 2
            r = rcopy(g.F.at[pl.ds(pl.multiple_of((1 - core) * n, 8), n)], out.at[:, cols], ess.at[e], ers.at[e], at.sib)
            l = pltpu.make_async_copy(g.F.at[pl.ds(pl.multiple_of(core * n, 8), n)], out.at[:, cols], els.at[e])
            r.start()
            l.start()
            finals.extend([r, l])

        def run(op, name=None, *arg):
            if op == GS:
                g_start(name)
            elif op == RF:
                f_out(name)
            elif op == ES:
                SE[0] = ge[...]
                sumE.start()
            elif op == E:
                sumE.middle()
            elif op < RS:
                g = gat[name]
                {GZ: g.step_z, GX: g.step_x, GY: g.step_y, GD: g.step_d, GC: g.share, GF: g.finish, GW: g.drain}[op](*arg)
            else:
                g = red[name]
                {RS: g.start, RC: g.step_c, RD: g.step_d, RX: g.step_xy, RZ: g.step_z}[op](*arg)

    else:
        ws = [pltpu.make_async_copy(a, b, ls.at[5 + i]) for i, (a, b) in enumerate(((wi_in, Wi), (wo_in, Wo), (wu_in, Wu), (wd_in, Wd)))]
        for c in ws:
            c.start()
        for c in ws:
            c.wait()

    def pump(*point):
        if comm:
            for step in SCHEDULE[point]:
                run(*step)

    pump(START)
    loads[0].wait()

    def norm_one(i, _):
        r = blk(i, RB)
        xh, _r = norm_parts(xa[r, :].astype(f32))
        h[r, :] = (xh * vec(vec_ref, "g1") + vec(vec_ref, "b1")).astype(bf)
        return 0

    lax.fori_loop(0, T // RB, norm_one, 0)
    loads[2].wait()

    def mask_rows(i, _):
        r = blk(i, RB)
        row = lax.broadcasted_iota(jnp.int32, (RB, 1), 0) + i * RB
        dy[r, :] = jnp.where(row < length, dy[r, :].astype(f32), 0.0).astype(bf)
        return 0

    lax.fori_loop(0, T // RB, mask_rows, 0)
    pump(NORM)

    eighth = jnp.asarray(0.125, bf)

    def project(group):
        fresh = group[0] < VH // 2
        c0 = PAIR * group[0]
        n = PAIR * len(group)
        qs, ks = slice(c0, c0 + n), slice(D + c0, D + c0 + n)

        def step(i, _):
            r = blk(i, RB * 2)
            hb = h[r, :]
            both = nn(hb, jnp.concatenate([Wi[:, qs], Wi[:, ks]], axis=1))
            q[r, qs] = (both[:, 0:n] + vec(vec_ref, "bq", c0, n)).astype(bf) * eighth
            k[r, qs] = both[:, n:].astype(bf)
            if fresh:
                vb = nn(hb, Wi[:, 2 * D : 2 * D + n]) + vec(vec_ref, "bv")
                v[r, qs] = vb.astype(bf)
            return 0

        lax.fori_loop(0, T // (RB * 2), step, 0)

    def pad_rows(i, _):
        r = blk(i, RB)
        row = lax.broadcasted_iota(jnp.int32, (RB, PAIR), 0) + i * RB
        lane = lax.broadcasted_iota(jnp.int32, (RB, PAIR), 1)
        pad[r, :] = jnp.where((lane == 0) & (row >= length), -1e9, 0.0).astype(bf)
        return 0

    lax.fori_loop(0, T // RB, pad_rows, 0)

    def scores(kp, qh, K):
        one = (lax.broadcasted_iota(jnp.int32, (QB, PAIR), 1) == 0).astype(f32).astype(bf)
        s = nt(kp, jnp.concatenate([qh, one], axis=1))
        key = lax.broadcasted_iota(jnp.int32, (QB, QB), 0)
        query = lax.broadcasted_iota(jnp.int32, (QB, QB), 1)
        last = jnp.where(key <= query, s[K - QB :], -1e9)
        return jnp.concatenate([s[0 : K - QB], last], axis=0) if K > QB else last

    def attend(p):
        c = blk(p, PAIR)
        vT = v[:, c].T
        for j in range(T // QB):
            if j != 1:
                pump(ATTEND, p, j)
            K = QB * (j + 1)
            rows = slice(QB * j, QB * j + QB)
            kp = jnp.concatenate([k[0:K, c], pad[0:K, :]], axis=1)
            for hd, qh in enumerate(halves(q[rows, c])):
                s = scores(kp, qh, K)
                top = jnp.max(s, axis=0, keepdims=True)
                e = jnp.exp(s - top)
                total = colsum(e)
                o = nn(vT[HD * hd : HD * hd + HD, 0:K], e.astype(bf))
                oT[pl.ds(pl.multiple_of(p * PAIR + HD * hd, HD), HD), rows] = (o / total).astype(bf)
                lse[2 * p + hd, :, rows] = top + jnp.log(total)

    loads[1].wait()
    for group in ((3,), (4,), (5,), (0, 1, 2)):
        pump(BEFORE_PROJECT, group[0])
        project(group)
        for p in group:
            attend(p)

    pump(BEFORE_OUT)

    def out_step(i, _):
        r = blk(i, RB)
        acc = xa[r, :].astype(f32) + vec(vec_ref, "bo") + tn(oT[:, r], Wo[...])
        h1[r, :] = acc
        xh, _r = norm_parts(acc)
        h2[r, :] = (xh * vec(vec_ref, "g2") + vec(vec_ref, "b2")).astype(bf)
        return 0

    lax.fori_loop(0, T // RB, out_step, 0)
    spill = pltpu.make_async_copy(h1, keep, ls.at[3])
    spill.start()
    unspill = pltpu.make_async_copy(keep, h1, ls.at[3])

    def put_early(name, value, at_=0):
        a = EARLY_AT[name] + at_
        ge[:, a : a + value.shape[1]] = value

    def put_late(name, value, at_=0):
        a = LATE_AT[name] + at_
        gl[:, a : a + value.shape[1]] = value

    for b in range(NB):
        pump(BEFORE_FFN, b)
        cu = slice(FB * b, FB * b + FB)
        if b == 0:
            spill.wait()

        def ffn(i, _, b=b, cu=cu):
            r = blk(i, FR)
            u = nn(h2[r, :], Wu[:, cu]) + vec(vec_ref, "bu", FB * b, FB)
            a, slope = gelu_both(u)
            ab = a.astype(bf)
            da = nt(dy[r, :], Wd[cu, :])
            dub = (slope * da).astype(bf)
            xa[r, :] = ab
            du[r, :] = dub
            feed = nn(ab, Wd[cu, :])
            if b < NB - 1:
                h1[r, :] += feed
            else:
                row = lax.broadcasted_iota(jnp.int32, (FR, 1), 0) + i * FR
                y = h1[r, :] + (feed + vec(vec_ref, "bd"))
                h1[r, :] = jnp.where(row < length, y, 0.0)
            back = nt(dub, Wu[:, cu])
            if b == 0:
                dh[r, :] = back
            else:
                dh[r, :] += back
            return 0

        lax.fori_loop(0, T // FR // 2, ffn, 0)
        pump(MID_FFN, b)
        lax.fori_loop(T // FR // 2, T // FR, ffn, 0)
        pump(BEFORE_DOWN, b)

        def down(i, _, b=b):
            r = blk(i, GR)
            Wd[pl.ds(pl.multiple_of(FB * b + i * GR, GR), GR), :] = tn(xa[:, r], dy[...]).astype(bf)
            return 0

        def up(i, _, cu=cu):
            r = blk(i, GR)
            Wu[r, cu] = tn(h2[:, r], du[...]).astype(bf)
            return 0

        lax.fori_loop(0, D // GR, down, 0)
        pump(BEFORE_UP, b)
        lax.fori_loop(0, D // GR, up, 0)
        pump(AFTER_UP, b)
        put_early("bu", colsum(du[...].astype(f32)), FB * b)

    def round_rows(i, _):
        r = blk(i, RB)
        xa[r, :] = h1[r, :].astype(bf)
        return 0

    lax.fori_loop(0, T // RB, round_rows, 0)
    unspill.start()
    res_out = pltpu.make_async_copy(xa, res, ls.at[4])
    res_out.start()
    pump(BEFORE_MID)
    unspill.wait()
    res_out.wait()

    def mid(i, carry):
        dg, db, dbo, dbd = carry
        r = blk(i, RB)
        xh, rs = norm_parts(h1[r, :])
        d = dh[r, :]
        dyf = dy[r, :].astype(f32)
        d1 = dyf + norm_back(d, vec(vec_ref, "g2"), xh, rs)
        dh[r, :] = d1
        da = d1.astype(bf)
        du[r, :] = da
        xa[r, :] = nt(da, Wo[...]).astype(bf)
        return dg + colsum(d * xh), db + colsum(d), dbo + colsum(da.astype(f32)), dbd + colsum(dyf)

    z = jnp.zeros((1, D), f32)
    sums = lax.fori_loop(0, T // RB, mid, (z, z, z, z))
    for name, value in zip(("g2", "b2", "bo", "bd"), sums):
        put_early(name, value)
    pump(BEFORE_GOUT)

    def gout(i, _):
        r = blk(i, RB)
        Go[r, :] = nn(oT[r, :], du[...]).astype(bf)
        return 0

    lax.fori_loop(0, D // RB, gout, 0)
    pump(AFTER_GOUT)

    def attend_back(p):
        c = blk(p, PAIR)
        kT = k[:, c].T
        for j in range(T // QB):
            if j != 1:
                pump(BACK, p, j)
            K = QB * (j + 1)
            L = K - QB
            rows = slice(QB * j, QB * j + QB)
            kp = jnp.concatenate([k[0:K, c], pad[0:K, :]], axis=1)
            qb, db = q[rows, c], xa[rows, c]
            qT, dT = qb.T, db.T
            dqs = []
            for hd, (qh, dhd) in enumerate(zip(halves(qb), halves(db))):
                hs = slice(HD * hd, HD * hd + HD)
                s = scores(kp, qh, K)
                pr = jnp.exp(s - lse[2 * p + hd, :, rows])
                dp = nt(v[0:K, c], dhd)
                inner = colsum(pr * dp)
                dsb = (pr * (dp - inner)).astype(bf)
                dqs.append(0.125 * nn(kT[hs, 0:K], dsb))
                dk = nt(qT[hs, :], dsb)
                dv = nt(dT[hs, :], pr.astype(bf))
                if j:
                    dkT[hs, 0:L] += dk[:, 0:L]
                    dvT[hs, 0:L] += dv[:, 0:L]
                dkT[hs, L:K] = dk[:, L:]
                dvT[hs, L:K] = dv[:, L:]
            h2[rows, c] = jnp.concatenate(dqs, axis=0).T.astype(bf)
        for j in range(T // QB):
            rows = slice(QB * j, QB * j + QB)
            dy[rows, c] = dkT[:, rows].T.astype(bf)
            du[rows, c] = dvT[:, rows].T.astype(bf)

    def gin(columns, parts):
        n = parts[0][1].stop - parts[0][1].start

        def step(i, _):
            r = blk(i, GR)
            g = tn(h[:, r], jnp.concatenate([src[:, s] for src, s in parts], axis=1)).astype(bf)
            for at_, c in enumerate(columns):
                Gi[r, c : c + n] = g[:, at_ * n : at_ * n + n]
            return 0

        lax.fori_loop(0, D // GR, step, 0)

    if comm:
        Gi[:, WIN:] = jnp.zeros((D, WPAD - WIN), bf)
    val_out = pltpu.make_async_copy(du.at[:, VH * HD :], gval, ls.at[1])
    for p in (3, 4, 5, 0, 1, 2):
        attend_back(p)
        if p == 5:
            val_out.start()
            pump(BEFORE_GIN, 3)
            s = slice(VH * HD, D)
            gin((VH * HD, D + VH * HD), ((h2, s), (dy, s)))
            pump(AFTER_GIN, 3)
        if p < VH // 2:
            s = slice(PAIR * p, PAIR * p + PAIR)
            pump(BEFORE_GIN, 10 + p)
            gin((PAIR * p, D + PAIR * p), ((h2, s), (dy, s)))
            pump(AFTER_GIN, 10 + p)
    pump(BEFORE_GIN_V)
    gin((2 * D,), ((du, slice(0, VH * HD)),))
    pump(AFTER_GIN_V)
    x_back = pltpu.make_async_copy(x_in, xa, ls.at[0])
    x_back.start()
    put_late("bq", colsum(h2[...].astype(f32)))
    put_late("bv", colsum(du[:, 0 : VH * HD].astype(f32)))
    x_back.wait()

    def last(i, carry):
        dg, db = carry
        r = blk(i, RB)
        d = nt(h2[r, :], Wi[:, 0:D]) + nt(dy[r, :], Wi[:, D : 2 * D]) + nt(du[r, 0 : VH * HD], Wi[:, 2 * D : WIN])
        xh, rs = norm_parts(xa[r, :].astype(f32))
        g = dh[r, :] + norm_back(d, vec(vec_ref, "g1"), xh, rs)
        xa[r, :] = g.astype(bf)
        return dg + colsum(d * xh), db + colsum(d)

    z2 = (z, z)
    for i in range(T // RB):
        pump(LAST, i)
        z2 = lax.fori_loop(i, i + 1, last, z2)
    put_late("g1", z2[0])
    put_late("b1", z2[1])
    tok_out = pltpu.make_async_copy(xa, gt, ls.at[0])
    tok_out.start()
    pump(TAIL)
    if comm:
        squares = jnp.zeros((1, 1), f32)
        for F in [Fi, Fv, Fo] + [Fa.at[i] for i in range(3)] + [Fu.at[b] for b in range(NB)] + [Fd]:
            f = F[...]
            squares = squares + jnp.sum(colsum(f * f), axis=1, keepdims=True)
        gl[:, LATE_N:] = jnp.broadcast_to(squares, (1, 128))
        SL[0] = gl[...]
        sumL.start()
        sumL.middle()
        gl[...] = sumL.last()
        ge[...] = sumE.last()
    else:
        gl[:, LATE_N:] = jnp.zeros((1, 128), f32)
    ends = [
        pltpu.make_async_copy(ge, ge_out, ls.at[2]),
        pltpu.make_async_copy(gl, gl_out, ls.at[3]),
    ]
    if not comm:
        for i, (a, o) in enumerate(((Gi, gi_out), (Go, go_out), (Wu, gu_out), (Wd, gd_out))):
            ends.append(pltpu.make_async_copy(a, o, ls.at[5 + i]))
    for e in ends:
        e.start()
    if comm:
        for f in finals:
            f.wait()
        for name in gat:
            if name <= O:
                gat[name].drain()
        for name in red:
            red[name].drain()
        sumE.drain()
        sumL.drain()
    for e in ends:
        e.wait()
    val_out.wait()
    tok_out.wait()


SCHEDULE = {
    (START,): ((GS, B3), (GS, B4), (GS, B5), (GS, A),),
    (NORM,): (),
    (BEFORE_PROJECT, 3,): ((GS, V), (GX, B3, 0), (GY, B3, 0), (GX, B4, 0), (GY, B4, 0), (GX, B5, 0), (GY, B5, 0), (GZ, B3, 3), (GX, A, 0), (GY, A, 0), (GZ, B3, 2), (GZ, B3, 1), (GS, D0), (GZ, B4, 3), (GZ, B4, 2), (GZ, B4, 1), (GZ, B5, 3), (GZ, B5, 2), (GZ, B5, 1), (GX, V, 0), (GY, V, 0), (GD, B3, 0), (GX, B3, 3), (GD, B4, 0), (GZ, A, 3), (GD, B5, 0), (GX, B3, 2), (GY, B3, 3), (GX, B3, 1), (GX, B4, 3), (GD, A, 0), (GX, B4, 2), (GY, B3, 2), (GX, B4, 1), (GZ, A, 2), (GY, B3, 1), (GX, B5, 3), (GY, B4, 3), (GY, B4, 2), (GX, B5, 2), (GZ, A, 1), (GY, B4, 1), (GX, B5, 1), (GY, B5, 3), (GZ, V, 3), (GY, B5, 2), (GY, B5, 1), (GS, O), (GZ, V, 2), (GD, V, 0), (GZ, V, 1), (GX, A, 3), (GY, A, 3), (GD, B3, 3), (GD, B3, 1), (GD, B3, 2), (GF, B3),),
    (ATTEND, 3, 0,): ((GD, B4, 1), (GD, B4, 2), (GD, B4, 3), (GX, A, 2), (GY, A, 2), (GY, A, 1),),
    (ATTEND, 3, 2,): ((GS, U0), (GD, B5, 1), (GD, B5, 2), (GD, B5, 3), (GX, A, 1), (GX, V, 3), (GY, V, 3), (GY, O, 0),),
    (ATTEND, 3, 3,): ((GY, V, 1), (GX, V, 2), (GY, V, 2), (GX, O, 0),),
    (BEFORE_PROJECT, 4,): ((GS, D1), (GD, A, 3), (GX, V, 1), (GZ, D0), (GF, B4),),
    (ATTEND, 4, 0,): ((GD, A, 2),),
    (ATTEND, 4, 2,): ((GZ, O, 3), (GX, U0, 0), (GY, U0, 0), (GD, V, 3),),
    (ATTEND, 4, 3,): ((GD, A, 1), (GD, V, 2), (GZ, O, 2), (GD, O, 0),),
    (BEFORE_PROJECT, 5,): ((GD, V, 1), (GZ, O, 1), (GF, B5),),
    (ATTEND, 5, 0,): ((GZ, U0, 3), (GS, U1),),
    (ATTEND, 5, 2,): ((GZ, U0, 2),),
    (ATTEND, 5, 3,): ((GX, D0), (GY, D0), (GX, O, 3), (GZ, U0, 1),),
    (BEFORE_PROJECT, 0,): ((GX, O, 2), (GY, O, 3), (GD, U0, 0), (GF, A), (GF, V),),
    (ATTEND, 0, 0,): ((GS, D2), (GX, O, 1), (GY, O, 1), (GY, O, 2), (GX, U0, 3), (GY, U0, 3), (GX, U1, 0), (GX, U0, 2),),
    (ATTEND, 0, 2,): ((GY, U0, 2), (GZ, D1), (GY, U1, 0),),
    (ATTEND, 0, 3,): ((GS, U2), (GD, D0), (GC, D0), (GX, U0, 1), (GZ, U1, 3),),
    (ATTEND, 1, 0,): ((GD, O, 3), (GY, U0, 1),),
    (ATTEND, 1, 2,): ((GS, D3), (GD, O, 1), (GD, O, 2), (GC, O), (GD, U0, 3), (GZ, U1, 1), (GZ, U1, 2), (GD, U1, 0), (GD, U0, 2),),
    (ATTEND, 1, 3,): (),
    (ATTEND, 2, 0,): (),
    (ATTEND, 2, 2,): ((GX, D1), (GY, D1), (GY, U2, 0),),
    (ATTEND, 2, 3,): ((GD, U0, 1), (GC, U0), (GZ, D2), (GX, U2, 0),),
    (BEFORE_OUT,): ((GX, U1, 1), (GY, U1, 1), (GX, U1, 3), (GY, U1, 3), (GZ, U2, 3), (GF, O),),
    (BEFORE_FFN, 0,): ((GS, U3), (GD, D1), (GC, D1), (GX, U1, 2), (GY, U1, 2), (GZ, U2, 1), (GZ, U2, 2), (GF, U0), (GF, D0),),
    (MID_FFN, 0,): ((GD, U1, 1), (GD, U1, 3), (GX, D2), (GY, D2), (GX, U2, 3), (GD, U2, 0), (GZ, D3),),
    (BEFORE_DOWN, 0,): ((GD, U1, 2), (GC, U1), (GX, U2, 1), (GY, U2, 1), (GY, U2, 2), (GY, U2, 3), (GZ, U3, 3), (GX, U3, 0), (GY, U3, 0), (GX, U2, 2), (GW, D0),),
    (BEFORE_UP, 0,): ((RS, D0), (GW, U0),),
    (AFTER_UP, 0,): ((GD, D2), (GC, D2), (GZ, U3, 2), (RS, U0), (GZ, U3, 1),),
    (BEFORE_FFN, 1,): ((GF, U1), (GF, D1),),
    (MID_FFN, 1,): ((GX, D3), (GY, D3),),
    (BEFORE_DOWN, 1,): ((GD, U2, 1), (GD, U2, 2), (GD, U2, 3), (GC, U2), (GX, U3, 2), (GY, U3, 2), (GX, U3, 3), (GY, U3, 3), (GD, U3, 0), (RC, D0), (GX, U3, 1), (GY, U3, 1), (GW, D1),),
    (BEFORE_UP, 1,): ((RS, D1), (GW, U1),),
    (AFTER_UP, 1,): ((GD, D3), (GC, D3), (RC, U0), (RS, U1),),
    (BEFORE_FFN, 2,): ((GF, U2), (GF, D2),),
    (MID_FFN, 2,): ((GD, U3, 2), (GD, U3, 3),),
    (BEFORE_DOWN, 2,): ((GD, U3, 1), (GC, U3), (RD, U0, 0), (RD, U0, 1), (RD, U0, 2), (RD, U0, 3), (RD, D0), (RC, D1), (GW, D2),),
    (BEFORE_UP, 2,): ((RS, D2), (RC, U1), (GW, U2),),
    (AFTER_UP, 2,): ((RS, U2),),
    (BEFORE_FFN, 3,): ((GF, U3), (GF, D3),),
    (MID_FFN, 3,): (),
    (BEFORE_DOWN, 3,): ((RX, U0, 1), (RX, U0, 2), (RX, U0, 3), (RX, U0, 0), (RC, U2), (RC, D2), (RX, D0), (GW, D3),),
    (BEFORE_UP, 3,): ((RD, D1), (RS, D3), (GW, U3),),
    (AFTER_UP, 3,): ((RD, U1, 0), (RD, U1, 2), (RS, U3),),
    (BEFORE_MID,): ((RD, U1, 3), (RD, U1, 1),),
    (BEFORE_GOUT,): ((RD, U2, 0), (RD, U2, 1), (RD, U2, 2), (RD, U2, 3), (RC, D3), (ES,), (RZ, U0), (RF, U0),),
    (AFTER_GOUT,): ((RD, D2), (RC, U3), (RS, O),),
    (BACK, 3, 0,): (),
    (BACK, 3, 2,): ((RX, D1),),
    (BACK, 3, 3,): ((RX, U1, 1), (RX, U1, 2), (RX, U1, 3), (RX, U1, 0),),
    (BACK, 4, 0,): ((RX, U2, 1), (RX, U2, 2), (RX, U2, 3), (RX, U2, 0),),
    (BACK, 4, 2,): ((RZ, D0), (RD, D3), (RC, O), (E,),),
    (BACK, 4, 3,): (),
    (BACK, 5, 0,): ((RX, D2), (RD, U3, 0), (RD, U3, 1), (RD, U3, 2),),
    (BACK, 5, 2,): ((RZ, D1), (RD, U3, 3),),
    (BACK, 5, 3,): (),
    (BEFORE_GIN, 3,): ((RZ, U1), (RF, U1), (RX, D3), (RD, O, 0),),
    (AFTER_GIN, 3,): ((RZ, U2), (RF, U2), (RD, O, 1), (RD, O, 2), (RD, O, 3), (RS, B),),
    (BACK, 0, 0,): (),
    (BACK, 0, 2,): (),
    (BACK, 0, 3,): ((RX, U3, 1), (RX, U3, 2), (RX, U3, 3), (RX, U3, 0),),
    (BEFORE_GIN, 10,): (),
    (AFTER_GIN, 10,): ((RX, O, 1), (RX, O, 2), (RX, O, 3), (RX, O, 0), (RC, B), (RS, A0), (RZ, D2),),
    (BACK, 1, 0,): (),
    (BACK, 1, 2,): (),
    (BACK, 1, 3,): (),
    (BEFORE_GIN, 11,): ((RC, A0), (RD, B, 0), (RD, B, 2),),
    (AFTER_GIN, 11,): ((RD, B, 1), (RD, B, 3), (RS, A1),),
    (BACK, 2, 0,): (),
    (BACK, 2, 2,): (),
    (BACK, 2, 3,): ((RZ, D3), (RF, D0), (RD, A0, 0), (RD, A0, 2),),
    (BEFORE_GIN, 12,): ((RZ, U3), (RF, U3), (RD, A0, 1), (RD, A0, 3), (RC, A1),),
    (AFTER_GIN, 12,): ((RX, B, 1), (RX, B, 2), (RX, B, 3), (RX, B, 0), (RS, A2),),
    (BEFORE_GIN_V,): (),
    (AFTER_GIN_V,): ((RZ, O), (RF, O), (RS, V),),
    (LAST, 0,): (),
    (LAST, 1,): ((RX, A0, 1), (RX, A0, 2), (RX, A0, 3), (RX, A0, 0), (RD, A1, 0), (RD, A1, 2),),
    (LAST, 2,): ((RD, A1, 1), (RD, A1, 3), (RC, A2),),
    (LAST, 3,): (),
    (TAIL,): ((RZ, B), (RF, B), (RC, V), (RZ, A0), (RF, A0), (RX, A1, 1), (RX, A1, 2), (RX, A1, 3), (RX, A1, 0), (RD, A2, 0), (RD, A2, 2), (RD, A2, 1), (RD, A2, 3), (RD, V, 0), (RD, V, 2), (RD, V, 1), (RD, V, 3), (RZ, A1), (RF, A1), (RX, A2, 1), (RX, A2, 2), (RX, A2, 3), (RX, A2, 0), (RX, V, 1), (RX, V, 2), (RX, V, 3), (RX, V, 0), (RZ, A2), (RF, A2), (RZ, V), (RF, V),),
}


def block(comm, length, x, fv, ct, vectors, wi, wo, wu, wd):
    T = x.shape[0]
    V, S = pltpu.VMEM, pltpu.SemaphoreType.DMA
    hbm = pl.BlockSpec(memory_space=pl.ANY)
    shape = jax.ShapeDtypeStruct
    outs = [shape((T, D), bf), shape((T, D), bf), shape((T, (H - VH) * HD), bf)]
    if comm:
        outs += [shape((24, WPAD), f32), shape((24, D), f32), shape((24, FF), f32), shape((96, D), f32)]
    else:
        outs += [shape((D, WPAD), bf), shape((D, D), bf), shape((D, FF), bf), shape((FF, D), bf)]
    outs += [shape((1, EARLY_N), f32), shape((1, LATE_ALL), f32), shape((T, D), f32)]
    row = lambda: V((T, D), bf)
    full = lambda: V((T, D), f32)
    scratch = [V((D, WPAD), bf), V((D, D), bf), V((D, FF), bf), V((FF, D), bf), V((D, WPAD), bf), V((D, D), bf)]
    scratch += [row(), row(), row(), row(), row(), row(), V((D, T), bf), V((H, 1, T), f32), full(), row(), full(), row()]
    scratch += [V((PAIR, T), f32), V((PAIR, T), f32), V((1, EARLY_N), f32), V((1, LATE_ALL), f32), V((T, PAIR), bf), S((9,))]
    params = dict(vmem_limit_bytes=63 << 20)
    if comm:
        scratch += [V((D, 384), bf), V((3, D, 128), bf), V((D, 256), bf), V((D, 384), bf), V((NB, D, 384), bf), V((NB, D, 384), bf)]
        scratch += [V((15, 48, 384), bf), V((3, 15, 48, 128), bf), V((15, 48, 256), bf), V((15, 48, 384), bf)]
        scratch += [V((NB, 15, 48, 384), bf), V((NB, 6, 192, 384), bf)]
        scratch += [V((48, 384), f32), V((3, 48, 128), f32), V((48, 256), f32), V((48, 384), f32), V((NB, 48, 384), f32), V((192, 384), f32)]
        scratch += [V((2, 24, WIN), f32), V((2, 24, D), f32), V((2, 24, FF), f32), V((2, 96, D), f32)]
        scratch += [V((2, 1, EARLY_N), f32), V((12, 1, EARLY_N), f32), V((2, 1, LATE_ALL), f32), V((12, 1, LATE_ALL), f32)]
        scratch += [S((14, NSLOT))] * 4 + [S((20,)), S((20,)), S((20,)), S((2, 11)), S((2, 11))]
        params.update(collective_id=1, has_side_effects=True)
    specs = [pl.BlockSpec(memory_space=pltpu.SMEM), hbm, hbm, hbm, pl.BlockSpec(memory_space=pltpu.VMEM), hbm, hbm, hbm, hbm]
    return pl.pallas_call(
        functools.partial(block_kernel, comm, T),
        out_shape=outs,
        in_specs=specs,
        out_specs=[hbm] * len(outs),
        scratch_shapes=scratch,
        compiler_params=pltpu.CompilerParams(**params),
    )(length, x, fv, ct, vectors, wi, wo, wu, wd)


def adam_step(master, grad, first, second, shadow, rate, decay):
    moment = BETA_ONE * first + (1.0 - BETA_ONE) * grad
    square = BETA_TWO * second + (1.0 - BETA_TWO) * grad * grad
    moment_hat = moment / (1.0 - BETA_ONE**STEP)
    square_hat = square / (1.0 - BETA_TWO**STEP)
    updated = master - rate * (moment_hat / (jnp.sqrt(square_hat) + EPS_ADAM) + decay * master)
    average = SHADOW_RATE * shadow + (1.0 - SHADOW_RATE) * updated
    return (updated, moment, square, average)


RATES = (RATE_MATRIX, RATE_OUTPUT, RATE_MATRIX, RATE_MATRIX)


def adam_kernel(*refs):
    ins, moved, norm, outs, moves, rest = refs[:26], refs[26:29], refs[29], refs[30:50], refs[50:53], refs[53:]
    bufs, news, isem, osem = rest[:26], rest[26:46], rest[46], rest[47]
    order = [4, 5] + [j for i in range(4) for j in (i, 6 + i, 10 + i, 14 + i, 18 + i)] + [22, 23, 24, 25]
    loads = {j: pltpu.make_async_copy(ins[j], bufs[j], isem.at[j]) for j in order}
    for j in order:
        loads[j].start()
    passing = [pltpu.make_async_copy(a, v, osem.at[23 + i]) for i, (a, v) in enumerate(zip(moved, rest[48:51]))]
    for c in passing:
        c.start()
    stores = []

    def send(i):
        c = pltpu.make_async_copy(news[i], outs[i], osem.at[i])
        c.start()
        stores.append(c)

    loads[4].wait()
    loads[5].wait()
    ge, gl = bufs[4], bufs[5]
    e, l = ge[...], gl[:, 0:LATE_N]
    total = gl[:, LATE_N : LATE_N + 1] + jnp.sum(e * e, axis=1, keepdims=True) + jnp.sum(l * l, axis=1, keepdims=True)
    size = jnp.sqrt(total)
    norm[...] = size
    factor = jnp.minimum(1.0, CLIP / size)
    for i in range(4):
        for j in (i, 6 + i, 10 + i, 14 + i, 18 + i):
            loads[j].wait()
        n, m = bufs[6 + i].shape
        for r in range(0, n, 24):
            rs = slice(r, r + 24)
            state = (bufs[10 + i][rs, :], bufs[14 + i][rs, :], bufs[18 + i][rs, :])
            new = adam_step(bufs[6 + i][rs, :], factor * bufs[i][rs, 0:m], *state, RATES[i], DECAY_MATRIX)
            for j, value in enumerate(new):
                news[4 * i + j][rs, :] = value
        for j in range(4):
            send(4 * i + j)
        if i < 3:
            passing[i].wait()
            c = pltpu.make_async_copy(rest[48 + i], moves[i], osem.at[20 + i])
            c.start()
            stores.append(c)
    for j in range(22, 26):
        loads[j].wait()
    for where, ref in ((EARLY_AT, ge), (LATE_AT, gl)):
        for name, a in where.items():
            o, n = OFF[name]
            w, m1, m2, avg = (bufs[j][o : o + n].reshape(1, n) for j in range(22, 26))
            new = adam_step(w, factor * ref[:, a : a + n], m1, m2, avg, RATE_VECTOR, 0.0)
            for j, value in enumerate(new):
                news[16 + j][o : o + n] = value.reshape(n)
    for j in range(16, 20):
        send(j)
    for c in stores:
        c.wait()


def adam(grads, ge, gl, masters, firsts, seconds, shadows, vecs, moved):
    shape = lambda a: jax.ShapeDtypeStruct(a.shape, f32)
    hbm = pl.BlockSpec(memory_space=pl.ANY)
    outs = [shape(m) for m in masters for _ in range(4)] + [shape(vecs[0])] * 4
    args = [*grads, ge, gl, *masters, *firsts, *seconds, *shadows, *vecs]
    return pl.pallas_call(
        adam_kernel,
        out_shape=[jax.ShapeDtypeStruct((1, 1), f32)] + outs + [jax.ShapeDtypeStruct(a.shape, a.dtype) for a in moved],
        in_specs=[hbm] * (len(args) + 3),
        out_specs=[pl.BlockSpec(memory_space=pltpu.VMEM)] + [hbm] * (len(outs) + 3),
        scratch_shapes=[pltpu.VMEM(a.shape, f32) for a in args]
        + [pltpu.VMEM(o.shape, f32) for o in outs]
        + [pltpu.SemaphoreType.DMA((26,)), pltpu.SemaphoreType.DMA((26,))]
        + [pltpu.VMEM(a.shape, a.dtype) for a in moved],
        compiler_params=pltpu.CompilerParams(vmem_limit_bytes=60 << 20),
    )(*args, *moved)


def body(own_links, *args):
    tokens, first_values, cotangent, lengths = args[:4]
    masters, firsts, seconds, shadows = args[4:8], args[8:12], args[12:16], args[16:20]
    vectors, first_vectors, second_vectors, shadow_vectors = vecs = args[20:24]
    both = ("wide", "narrow")
    slots = tokens.shape[0]
    if own_links and slots == 1:
        got = block(True, lengths, tokens[0], first_values[0], cotangent[0], vectors, *masters)
        new = adam(got[3:7], got[7], got[8], masters, firsts, seconds, shadows, vecs, got[:3])
        return (*(a[None] for a in new[21:24]), new[0].reshape(()), *new[1:21])
    weights = [lax.all_gather(m.astype(bf), both, axis=0, tiled=True) for m in masters]
    weights[0] = jnp.pad(weights[0], ((0, 0), (0, WPAD - WIN)))
    per_slot = [
        block(False, lengths[i : i + 1], tokens[i], first_values[i], cotangent[i], vectors, *weights) for i in range(slots)
    ]
    result, grad_tokens, grad_values = (jnp.stack([s[i] for s in per_slot]) for i in range(3))
    totals = [sum(s[i].astype(f32) for s in per_slot) for i in range(3, 9)]
    totals[0] = totals[0][:, :WIN]
    shards = [lax.psum_scatter(g, both, scatter_dimension=0, tiled=True) for g in totals[:4]]
    squares = sum(jnp.sum(g * g) for g in shards)
    pieces = {n: totals[4][0, a : a + OFF[n][1]] for n, a in EARLY_AT.items()}
    pieces.update({n: totals[5][0, a : a + OFF[n][1]] for n, a in LATE_AT.items()})
    vector_grad, squares = lax.psum((jnp.concatenate([pieces[n] for n in OFF]), squares), both)
    grad_norm = jnp.sqrt(squares + jnp.sum(vector_grad * vector_grad))
    factor = jnp.minimum(1.0, CLIP / grad_norm)
    outputs = [result, grad_tokens, grad_values, grad_norm]
    for i in range(4):
        outputs.extend(adam_step(masters[i], factor * shards[i], firsts[i], seconds[i], shadows[i], RATES[i], DECAY_MATRIX))
    outputs.extend(adam_step(vectors, factor * vector_grad, first_vectors, second_vectors, shadow_vectors, RATE_VECTOR, 0.0))
    return tuple(outputs)


def solution(mesh):
    both = ("wide", "narrow")
    rows3, rows2 = P(both, None, None), P(both, None)
    own_links = (mesh.shape["wide"], mesh.shape["narrow"]) == (8, 4)
    return jax.shard_map(
        functools.partial(body, own_links),
        mesh=mesh,
        in_specs=(rows3,) * 3 + (P(both),) + (rows2,) * 16 + (P(),) * 4,
        out_specs=(rows3,) * 3 + (P(),) + (rows2,) * 16 + (P(),) * 4,
        check_vma=False,
    )
```
